32 devices in a mesh: dp: 4 (over y, x), tensor: 8 (over z, core).
Axes of the slice: x: 2, y: 2, z: 4, core: 2. Of those that a mesh axis runs over, the one named last changes fastest.
Arguments:
- tokens: bfloat16 [4096, 4096], P(('dp', 'tensor')), may hold values from -6 to 6
- panel: bfloat16 [4096, 1024], P('tensor'), may hold values from -0.09375 to 0.09375
- cotangent: bfloat16 [4096, 512], P(('dp', 'tensor')), may hold values from -6 to 6
Outputs:
- hidden: float32 [4096, 512], P(('dp', 'tensor'))
- grad_panel: float32 [4096, 1024], P('tensor')
The draws below stay inside these ranges and needn't reach their ends.
All inputs are finite; a program needn't handle non-finite values.
Results may differ from the reference program's by a relative error of at most 0.015.
Values may be sent and summed in bfloat16 or wider, within the bound.
A program may use at most 64 MiB of HBM per device.

```python
import jax
import jax.numpy as jnp
from jax import lax

D = 4096
H = 512
TOK_DEV = 128
TOKENS = 4096
N_DP = 4
N_TENSOR = 8


def raised(entries, own_key, source, target, shards_of, factor):
    owner, partner = [(jnp.arange(entries.shape[position]) // (entries.shape[position] // shards_of)).reshape([-1 if axis == position else 1 for axis in range(entries.ndim)]) for position in (source, target)]
    chosen = jax.random.permutation(own_key, shards_of)[partner]
    strong = (owner == chosen) | (owner == (partner + shards_of // 2) % shards_of)
    return jnp.where(strong, factor * entries, entries)


def block_scale(key, shape, pieces, smallest, largest):
    factor_of = 1.0
    for position, shards_of in pieces:
        heights = jax.random.uniform(jax.random.fold_in(jax.random.fold_in(key, 6), position), (shards_of,), jnp.float32, smallest / len(pieces), largest / len(pieces))
        factor_of = factor_of * jnp.repeat(jnp.exp(heights), shape[position] // shards_of).reshape((-1,) + (1,) * (len(shape) - 1 - position))
    return factor_of


def gaussian(rng, extent, scale, reach, shards=(), held_as=jnp.bfloat16):
    result = jax.random.normal(rng, extent, jnp.float32) * scale
    if len(shards) > 0:
        result = block_scale(rng, extent, shards, -0.22, 0.18) * result
    return jnp.clip(result, min=-reach, max=reach).astype(held_as)


def heavy_noise(key, extent, deviation, reach, pieces, heavy, kind=jnp.bfloat16):
    array = deviation * jax.random.normal(key, extent, jnp.float32)
    if pieces:
        array = array * block_scale(key, extent, pieces, -0.22, 0.18)
    return jnp.clip(raised(array, jax.random.fold_in(key, 3), *heavy), -reach, reach).astype(kind)


def setup_inputs(seed: int = 0) -> dict:
    arg_keys = jax.random.split(jax.random.key(seed), 4)
    return {
        "tokens": heavy_noise(arg_keys[0], (TOKENS, D), 1.0, 6.0, ((0, 32),), (0, 1, 32, 2.75)),
        "panel": gaussian(arg_keys[1], (D, 2 * H), D ** -0.5, 0.09375, ((0, 8),)),
        "cotangent": gaussian(arg_keys[2], (TOKENS, H), 1.0, 6.0, ((0, 32),)),
    }


def reference(tokens, panel, cotangent):
    projected = jnp.dot(tokens, panel, preferred_element_type=jnp.float32)
    gate_pre = projected[:, :H]
    up_pre = projected[:, H:]
    sigmoid_gate = jax.nn.sigmoid(gate_pre)
    hidden = gate_pre * sigmoid_gate * up_pre
    grad_out = cotangent.astype(jnp.float32)
    gate_grad = grad_out * up_pre * sigmoid_gate * (1.0 + gate_pre * (1.0 - sigmoid_gate))
    up_grad = grad_out * gate_pre * sigmoid_gate
    pre_grad = jnp.concatenate([gate_grad, up_grad], axis=1).astype(jnp.bfloat16)
    scale = 1.0 / jnp.sqrt(jnp.float32(TOKENS))
    blocks_tok = tokens.reshape(N_DP * N_TENSOR, TOK_DEV, D)
    blocks_grad = pre_grad.reshape(N_DP * N_TENSOR, TOK_DEV, 2 * H)

    def add_block(running, pair):
        block_tok, block_grad = pair
        grad_term = lax.dot_general(block_tok, block_grad, (((0,), (0,)), ((), ())), preferred_element_type=jnp.float32) * scale
        rounded = lax.optimization_barrier(grad_term.astype(jnp.bfloat16))
        return (running + rounded.astype(jnp.float32), None)
    grad_panel, unused = lax.scan(add_block, jnp.zeros((D, 2 * H), jnp.float32), (blocks_tok, blocks_grad))
    return (hidden, grad_panel)
```

```python
import functools
import math

import jax
import jax.numpy as jnp
from jax import lax
from jax.experimental import pallas as pl
from jax.experimental.pallas import tpu as pltpu
from jax.sharding import PartitionSpec as P

MESH = pl.DeviceIdType.MESH
PARTS = 2


def repeat(low, high, body):
    if high - low <= 4:
        for i in range(low, high):
            body(i)
    else:
        lax.fori_loop(low, high, lambda i, carry: (body(i), carry)[1], 0)


def factor(n):
    return max(f for f in range(1, math.isqrt(n) + 1) if n % f == 0)


def kernel(
    n_dp, n_tensor, scale,
    tokens, panel, cotangent,
    hidden, grad,
    full, tok_all, tok_t, pre_all, acc, out_part, in_part,
    f1_s, f1_r, row_s, row_r, col_s, col_r, d0_s, d0_r, d1_s, d1_r, sib_s, sib_r,
    tok_s, tok_r, pre_s, pre_r, pair_s, pair_r, rs_s, rs_r, ag_s, ag_r,
):
    n_tok, _ = tokens.shape
    depth, cols = panel.shape
    units = cols // 2
    width = cols // PARTS
    n_z = n_tensor // 2
    n_b = factor(n_dp)
    n_a = n_dp // n_b
    d, t = lax.axis_index("dp"), lax.axis_index("tensor")
    a, b = d // n_b, d % n_b
    z, c = t // 2, t % 2
    pair = z * 2 + 1 - c

    chunk_rows = max(16, depth // n_dp)
    down = depth // chunk_rows
    across = n_dp // down

    def chunk(i, span, half=None):
        wide = span // across
        row = pl.multiple_of((i // across) * chunk_rows, chunk_rows)
        start = (i % across) * wide
        if half is not None:
            wide = wide // 2
            start = start + half * wide
        return pl.ds(row, chunk_rows), pl.ds(pl.multiple_of(start, wide), wide)

    def send(src, dst, s, r, dp, tensor):
        return pltpu.make_async_remote_copy(
            src_ref=src, dst_ref=dst, send_sem=s, recv_sem=r,
            device_id=(dp, tensor), device_id_type=MESH,
        )

    def blk(k):
        return ((z - k + n_z) % n_z) * 2 + c

    def far(k, core):
        return ((z + k) % n_z) * 2 + core

    def f1(k, src_blk=None):
        where = chunk(d, cols)
        own = t if src_blk is None else src_blk
        return send(panel.at[where], full.at[(own,) + where], f1_s.at[k], f1_r.at[k], d, far(k, c))

    def piece(k, i, s, r, to, half=None):
        ref = full.at[(blk(k),) + chunk(i, cols, half)]
        return send(ref, ref, s.at[k], r.at[k], to, t)

    def a_peer(i):
        return ((a + i + n_a) % n_a) * n_b + b

    def b_peer(j):
        return a * n_b + (b + j + n_b) % n_b

    def ab_peer(i, j):
        return ((a + i + n_a) % n_a) * n_b + (b + j + n_b) % n_b

    def sib(k):
        src = panel if isinstance(k, int) and k == 0 else full.at[blk(k)]
        return send(src, full.at[blk(k)], sib_s.at[k], sib_r.at[k], d, pair)

    def tok(k, other):
        to = far(k, (1 - c) if other else c)
        src = tokens.at[:, pl.ds(pl.multiple_of(to * depth, depth), depth)]
        return send(src, tok_all.at[t], tok_s.at[k, other], tok_r.at[k, other], d, to)

    def rows_of(i):
        return pl.ds(pl.multiple_of(i * n_tok, n_tok), n_tok)

    def pre(h, k, own):
        ref = pre_all.at[h, rows_of(own)]
        return send(ref, ref, pre_s.at[h, k], pre_r.at[h, k], d, far(k, c))

    def pre_pair(h, k):
        ref = pre_all.at[h, rows_of(blk(k))]
        return send(ref, ref, pair_s.at[h, k], pair_r.at[h, k], d, pair)

    def rs(h, j):
        to = (d + j) % n_dp
        return send(out_part.at[h, to], in_part.at[h, j], rs_s.at[h, j], rs_r.at[h, j], to, t)

    def place(h, i):
        row, col = chunk(i, width)
        return row, pl.ds(pl.multiple_of(h * width + col.start, col.size), col.size)

    def ag(h, j, i):
        ref = grad.at[place(h, i)]
        return send(ref, ref, ag_s.at[h, j], ag_r.at[h, j], (d + j) % n_dp, t)

    barrier = pltpu.get_barrier_semaphore()

    def greet_tensor(k):
        pl.semaphore_signal(barrier, inc=1, device_id=(d, (t + k) % n_tensor), device_id_type=MESH)

    def greet_dp(k):
        pl.semaphore_signal(barrier, inc=1, device_id=((d + k) % n_dp, t), device_id_type=MESH)

    repeat(1, n_tensor, greet_tensor)
    repeat(1, n_dp, greet_dp)
    pl.semaphore_wait(barrier, n_tensor + n_dp - 2)

    repeat(1, n_z, lambda k: f1(k).start())
    sib(0).start()
    tok(0, 1).start()

    def multiply(own, ref):
        x = tokens[:, pl.ds(pl.multiple_of(own * depth, depth), depth)]
        return jnp.dot(x, ref[...], preferred_element_type=jnp.float32)

    acc[...] = multiply(t, panel)

    def spread(k):
        f1(k, blk(k)).wait_recv()
        repeat(1, n_b, lambda j: piece(k, d, row_s, row_r, b_peer(j)).start())
        repeat(1, n_a, lambda i: piece(k, d, col_s, col_r, a_peer(i)).start())
        tok(k, 0).start()
        tok(k, 1).start()

    def relay(k):
        repeat(1, n_b, lambda j: piece(k, b_peer(-j), row_s, row_r, d).wait_recv())

        def pass_a(j):
            repeat(1, n_a, lambda i: piece(k, b_peer(-j), d0_s, d0_r, a_peer(i), 0).start())

        repeat(1, n_b, pass_a)
        repeat(1, n_a, lambda i: piece(k, a_peer(-i), col_s, col_r, d).wait_recv())

        def pass_b(i):
            repeat(1, n_b, lambda j: piece(k, a_peer(-i), d1_s, d1_r, b_peer(j), 1).start())

        repeat(1, n_a, pass_b)

    def finish(k):
        def corner(i):
            def corner_b(j):
                piece(k, ab_peer(-i, -j), d0_s, d0_r, d, 0).wait_recv()
                piece(k, ab_peer(-i, -j), d1_s, d1_r, d, 1).wait_recv()
            repeat(1, n_b, corner_b)
        repeat(1, n_a, corner)
        sib(k).start()
        acc[...] += multiply(blk(k), full.at[blk(k)])

    def other(k):
        own = ((z - k + n_z) % n_z) * 2 + 1 - c
        dst = full.at[own]
        send(dst, dst, sib_s.at[k], sib_r.at[k], d, pair).wait_recv()
        acc[...] += multiply(own, dst)

    def when(k, body):
        if isinstance(k, int):
            if 1 <= k < n_z:
                body(k)
        else:
            pl.when((k >= 1) & (k < n_z))(lambda: body(k))

    def stage(k):
        when(k, spread)
        when(k - 1, relay)
        when(k - 2, finish)
        when(k - 3, other)

    for k in range(1, min(n_z, 4)):
        stage(k)
        if k == 1:
            other(0)
    if n_z > 4:
        lax.fori_loop(4, n_z, lambda k, carry: (stage(k), carry)[1], 0)
    for k in range(n_z, n_z + 3):
        stage(k)

    gate = acc[:, :units]
    up = acc[:, units:]
    s = jax.nn.sigmoid(gate)
    act = gate * s
    hidden[...] = act * up
    ct = cotangent[...].astype(jnp.float32)
    gate_grad = ct * up * s * (1.0 + gate * (1.0 - s))
    pre_all[0, rows_of(t), :] = gate_grad.astype(jnp.bfloat16)
    pre_all[1, rows_of(t), :] = (ct * act).astype(jnp.bfloat16)

    for h in range(PARTS):
        repeat(1, n_z, lambda k: pre(h, k, t).start())
        pre_pair(h, 0).start()

    tok_t[:, rows_of(t)] = tokens[:, pl.ds(pl.multiple_of(t * depth, depth), depth)].T

    def take(own, k, index):
        dst = tok_all.at[own]
        send(dst, dst, tok_s.at[k, index], tok_r.at[k, index], d, pair).wait_recv()
        tok_t[:, rows_of(own)] = dst[...].T

    take(pair, 0, 1)

    def take_both(k):
        take(blk(k), k, 0)
        take(((z - k + n_z) % n_z) * 2 + 1 - c, k, 1)

    repeat(1, n_z, take_both)

    def reduced(h):
        repeat(1, n_dp, lambda j: rs(h, j).wait_recv())
        total = out_part[h, d].astype(jnp.float32)
        for j in range(1, n_dp):
            total = total + in_part[h, j].astype(jnp.float32)
        grad[place(h, d)] = total.astype(jnp.bfloat16)
        repeat(1, n_dp, lambda j: ag(h, j, d).start())

    for h in range(PARTS):
        def arrive(k):
            pre(h, k, blk(k)).wait_recv()
            pre_pair(h, k).start()

        def arrive_pair(k):
            own = ((z - k + n_z) % n_z) * 2 + 1 - c
            ref = pre_all.at[h, rows_of(own)]
            send(ref, ref, pair_s.at[h, k], pair_r.at[h, k], d, pair).wait_recv()

        repeat(1, n_z, arrive)
        repeat(0, n_z, arrive_pair)
        def product(i):
            row, col = chunk(i, width)
            term = jnp.dot(tok_t[row, :], pre_all[h, :, col], preferred_element_type=jnp.float32)
            out_part[h, i] = (term * scale).astype(jnp.bfloat16)

        repeat(0, n_dp, product)
        repeat(1, n_dp, lambda j: rs(h, j).start())
        reduced(h)

    for h in range(PARTS):
        repeat(1, n_dp, lambda j: ag(h, j, (d - j + n_dp) % n_dp).wait_recv())

    def sent(k):
        f1(k).wait_send()
        repeat(1, n_b, lambda j: piece(k, d, row_s, row_r, b_peer(j)).wait_send())
        repeat(1, n_a, lambda i: piece(k, d, col_s, col_r, a_peer(i)).wait_send())

        def corner(i):
            def corner_b(j):
                piece(k, b_peer(-j), d0_s, d0_r, a_peer(i), 0).wait_send()
                piece(k, a_peer(-i), d1_s, d1_r, b_peer(j), 1).wait_send()
            repeat(1, n_b, corner_b)
        repeat(1, n_a, corner)
        sib(k).wait_send()
        tok(k, 0).wait_send()
        tok(k, 1).wait_send()
        for h in range(PARTS):
            pre(h, k, t).wait_send()
            pre_pair(h, k).wait_send()

    repeat(1, n_z, sent)
    sib(0).wait_send()
    tok(0, 1).wait_send()
    for h in range(PARTS):
        pre_pair(h, 0).wait_send()
        repeat(1, n_dp, lambda j: rs(h, j).wait_send())
        repeat(1, n_dp, lambda j: ag(h, j, d).wait_send())


def on_device(tokens, panel, cotangent):
    n_tok, depth_all = tokens.shape
    depth, cols = panel.shape
    n_tensor = lax.axis_size("tensor")
    n_dp = lax.axis_size("dp")
    n_z = n_tensor // 2
    scale = 1.0 / math.sqrt(n_tok * n_tensor * n_dp)
    chunk_rows = max(16, depth // n_dp)
    across = n_dp // (depth // chunk_rows)
    part = (PARTS, n_dp, chunk_rows, cols // PARTS // across)
    dma = pltpu.SemaphoreType.DMA
    vmem = pl.BlockSpec(memory_space=pltpu.VMEM)
    flops = 4 * n_tok * depth_all * cols
    hidden, grad = pl.pallas_call(
        functools.partial(kernel, n_dp, n_tensor, scale),
        out_shape=(
            jax.ShapeDtypeStruct((n_tok, cols // 2), jnp.float32),
            jax.ShapeDtypeStruct((depth, cols), jnp.bfloat16),
        ),
        in_specs=[vmem] * 3,
        out_specs=(vmem, vmem),
        scratch_shapes=[
            pltpu.VMEM((n_tensor, depth, cols), jnp.bfloat16),
            pltpu.VMEM((n_tensor, n_tok, depth), jnp.bfloat16),
            pltpu.VMEM((depth, n_tensor * n_tok), jnp.bfloat16),
            pltpu.VMEM((PARTS, n_tensor * n_tok, cols // PARTS), jnp.bfloat16),
            pltpu.VMEM((n_tok, cols), jnp.float32),
            pltpu.VMEM(part, jnp.bfloat16),
            pltpu.VMEM(part, jnp.bfloat16),
        ]
        + [dma((n_z,))] * 12
        + [dma((n_z, 2))] * 2
        + [dma((PARTS, n_z))] * 4
        + [dma((PARTS, n_dp))] * 4,
        compiler_params=pltpu.CompilerParams(
            collective_id=0, has_side_effects=True, vmem_limit_bytes=48 * 1024 * 1024
        ),
        cost_estimate=pl.CostEstimate(
            flops=flops, bytes_accessed=4 * depth * cols, transcendentals=n_tok * cols // 2
        ),
    )(tokens, panel, cotangent)
    return hidden, grad.astype(jnp.float32)


def solution(mesh):
    placed = (P(("dp", "tensor"), None), P("tensor", None), P(("dp", "tensor"), None))
    return jax.shard_map(
        on_device,
        mesh=mesh,
        in_specs=placed,
        out_specs=(P(("dp", "tensor"), None), P("tensor", None)),
        check_vma=False,
    )
```

```python
import functools
import math

import jax
import jax.numpy as jnp
from jax import lax
from jax.experimental import pallas as pl
from jax.experimental.pallas import tpu as pltpu
from jax.sharding import PartitionSpec as P

MESH = pl.DeviceIdType.MESH
LANES = 128


def repeat(low, high, body):
    if high - low <= 4:
        for i in range(low, high):
            body(i)
    else:
        lax.fori_loop(low, high, lambda i, carry: (body(i), carry)[1], 0)


def factor(n):
    return max(f for f in range(1, math.isqrt(n) + 1) if n % f == 0)


def kernel(
    n_dp, n_tensor, parts, scale,
    tokens, panel, cotangent,
    hidden, grad,
    tok_v, ct_v, hid_v, full, tok_all, tok_t, pre_all, acc, out_part, in_part, sum_v,
    in_sem, f1_s, f1_r, row_s, row_r, col_s, col_r, d0_s, d0_r, d1_s, d1_r, sib_s, sib_r,
    pair_s, pair_r, pre_s, pre_r, own_s, preo_s, tok_s, tok_r, rs_s, rs_r, ag_s, ag_r,
):
    n_tok, _ = tokens.shape
    depth, cols = panel.shape
    units = cols // 2
    width = cols // parts
    n_z = n_tensor // 2
    n_b = factor(n_dp)
    n_a = n_dp // n_b
    d, t = lax.axis_index("dp"), lax.axis_index("tensor")
    a, b = d // n_b, d % n_b
    z, c = t // 2, t % 2
    pair = z * 2 + 1 - c

    chunk_rows = max(16, depth // n_dp)
    down = depth // chunk_rows
    across = n_dp // down

    def chunk(i, span, half=None):
        wide = span // across
        row = pl.multiple_of((i // across) * chunk_rows, chunk_rows)
        start = (i % across) * wide
        if half is not None:
            wide = wide // 2
            start = start + half * wide
        return pl.ds(row, chunk_rows), pl.ds(pl.multiple_of(start, wide), wide)

    def send(src, dst, s, r, dp, tensor):
        return pltpu.make_async_remote_copy(
            src_ref=src, dst_ref=dst, send_sem=s, recv_sem=r,
            device_id=(dp, tensor), device_id_type=MESH,
        )

    def at_z(place, core):
        return place * 2 + core

    def arrival(n):
        short = jnp.minimum(z, n_z - 1 - z)
        both = n < 2 * short
        m = jnp.where(both, n // 2 + 1, n - short + 1)
        side = jnp.where(both, 2 * (n % 2) - 1, jnp.where(z > n_z - 1 - z, -1, 1))
        return z + side * m, z - side

    def inside(place):
        return (place >= 0) & (place < n_z)

    def f1_own(way):
        where = chunk(d, cols)
        to = at_z(z + 2 * way - 1, c)
        return send(panel.at[where], full.at[(t,) + where], own_s.at[way], f1_r.at[z], d, to)

    def f1(src, to):
        ref = full.at[(at_z(src, c),) + chunk(d, cols)]
        return send(ref, ref, f1_s.at[src], f1_r.at[src], d, at_z(to, c))

    def piece(src, i, s, r, to, half=None):
        ref = full.at[(at_z(src, c),) + chunk(i, cols, half)]
        return send(ref, ref, s.at[src], r.at[src], to, t)

    def a_peer(i):
        return ((a + i + n_a) % n_a) * n_b + b

    def b_peer(j):
        return a * n_b + (b + j + n_b) % n_b

    def ab_peer(i, j):
        return ((a + i + n_a) % n_a) * n_b + (b + j + n_b) % n_b

    def sib_own():
        return send(panel, full.at[t], sib_s.at[z], sib_r.at[z], d, pair)

    def sib(src, core):
        ref = full.at[at_z(src, core)]
        return send(ref, ref, sib_s.at[src], sib_r.at[src], d, pair)

    def far(k, core):
        return at_z((z + k + n_z) % n_z, core)

    def columns_of(i):
        return pl.ds(pl.multiple_of(i * depth, depth), depth)

    def rows_of(i):
        return pl.ds(pl.multiple_of(i * n_tok, n_tok), n_tok)

    def tok(k, other):
        to = far(k, (1 - c) if other else c)
        return send(
            tok_v.at[:, columns_of(to)], tok_all.at[t], tok_s.at[k, other], tok_r.at[k, other], d, to
        )

    def pre_own(p, way):
        ref = pre_all.at[p, rows_of(t)]
        to = at_z(z + 2 * way - 1, c)
        return send(ref, ref, preo_s.at[p, way], pre_r.at[p, z], d, to)

    def pre(p, src, to):
        ref = pre_all.at[p, rows_of(at_z(src, c))]
        return send(ref, ref, pre_s.at[p, src], pre_r.at[p, src], d, at_z(to, c))

    def pre_pair(p, src, core):
        ref = pre_all.at[p, rows_of(at_z(src, core))]
        return send(ref, ref, pair_s.at[p, src], pair_r.at[p, src], d, pair)

    def rs(p, j):
        to = (d + j) % n_dp
        return send(out_part.at[p, to], in_part.at[p, j], rs_s.at[p, j], rs_r.at[p, j], to, t)

    def place(p, i):
        row, col = chunk(i, width)
        return row, pl.ds(pl.multiple_of(p * width + col.start, col.size), col.size)

    def ag(p, j, i):
        return send(
            sum_v.at[p], grad.at[place(p, i)], ag_s.at[p, j], ag_r.at[p, j], (d + j) % n_dp, t
        )

    def both_ways(copy, act):
        pl.when(z > 0)(lambda: act(copy(0)))
        pl.when(z < n_z - 1)(lambda: act(copy(1)))

    def start(copy):
        copy.start()

    def gone(copy):
        copy.wait_send()

    tokens_in = pltpu.make_async_copy(tokens, tok_v, in_sem.at[0])
    panel_in = pltpu.make_async_copy(panel, full.at[t], in_sem.at[1])
    ct_in = pltpu.make_async_copy(cotangent, ct_v, in_sem.at[2])
    tokens_in.start()
    panel_in.start()
    ct_in.start()

    barrier = pltpu.get_barrier_semaphore()

    def greet_tensor(k):
        pl.semaphore_signal(barrier, inc=1, device_id=(d, (t + k) % n_tensor), device_id_type=MESH)

    def greet_dp(k):
        pl.semaphore_signal(barrier, inc=1, device_id=((d + k) % n_dp, t), device_id_type=MESH)

    repeat(1, n_tensor, greet_tensor)
    repeat(1, n_dp, greet_dp)
    pl.semaphore_wait(barrier, n_tensor + n_dp - 2)

    both_ways(f1_own, start)
    sib_own().start()
    tokens_in.wait()
    panel_in.wait()
    ct_in.wait()
    tok(0, 1).start()

    def multiply(own):
        return jnp.dot(tok_v[:, columns_of(own)], full[own], preferred_element_type=jnp.float32)

    acc[...] = multiply(t)

    def spread(n):
        src, to = arrival(n)
        f1(src, to).wait_recv()
        pl.when(inside(to))(lambda: f1(src, to).start())
        repeat(1, n_b, lambda j: piece(src, d, row_s, row_r, b_peer(j)).start())
        repeat(1, n_a, lambda i: piece(src, d, col_s, col_r, a_peer(i)).start())
        tok(n + 1, 0).start()
        tok(n + 1, 1).start()

    def relay(n):
        src, _ = arrival(n)
        repeat(1, n_b, lambda j: piece(src, b_peer(-j), row_s, row_r, d).wait_recv())

        def pass_a(j):
            repeat(1, n_a, lambda i: piece(src, b_peer(-j), d0_s, d0_r, a_peer(i), 0).start())

        repeat(1, n_b, pass_a)
        repeat(1, n_a, lambda i: piece(src, a_peer(-i), col_s, col_r, d).wait_recv())

        def pass_b(i):
            repeat(1, n_b, lambda j: piece(src, a_peer(-i), d1_s, d1_r, b_peer(j), 1).start())

        repeat(1, n_a, pass_b)

    def finish(n):
        src, _ = arrival(n)

        def corner(i):
            def corner_b(j):
                piece(src, ab_peer(-i, -j), d0_s, d0_r, d, 0).wait_recv()
                piece(src, ab_peer(-i, -j), d1_s, d1_r, d, 1).wait_recv()
            repeat(1, n_b, corner_b)
        repeat(1, n_a, corner)
        sib(src, c).start()
        acc[...] += multiply(at_z(src, c))

    def other(src):
        sib(src, 1 - c).wait_recv()
        acc[...] += multiply(at_z(src, 1 - c))

    def when(n, body):
        if isinstance(n, int):
            if 0 <= n < n_z - 1:
                body(n)
        else:
            pl.when((n >= 0) & (n < n_z - 1))(lambda: body(n))

    def stage(n):
        when(n, spread)
        when(n - 1, relay)
        when(n - 2, finish)
        when(n - 3, lambda m: other(arrival(m)[0]))

    stage(0)
    other(z)
    repeat(1, n_z + 2, stage)

    gate = acc[:, :units]
    up = acc[:, units:]
    s = jax.nn.sigmoid(gate)
    act = gate * s
    ct = ct_v[...].astype(jnp.float32)
    gate_grad = (ct * up * s * (1.0 + gate * (1.0 - s))).astype(jnp.bfloat16)
    up_grad = (ct * act).astype(jnp.bfloat16)
    for p in range(parts):
        term = gate_grad if p < parts // 2 else up_grad
        first = (p % (parts // 2)) * width
        pre_all[p, rows_of(t), :] = term[:, first:first + width]
        if p < 2:
            both_ways(lambda way: pre_own(p, way), start)
            pre_pair(p, z, c).start()
    hid_v[...] = act * up
    hidden_out = pltpu.make_async_copy(hid_v, hidden, in_sem.at[3])
    hidden_out.start()

    tok_t[:, rows_of(t)] = tok_v[:, columns_of(t)].T

    def take(own, k, index):
        dst = tok_all.at[own]
        send(dst, dst, tok_s.at[k, index], tok_r.at[k, index], d, pair).wait_recv()
        tok_t[:, rows_of(own)] = dst[...].T

    take(pair, 0, 1)

    def take_both(k):
        take(far(-k, c), k, 0)
        take(far(-k, 1 - c), k, 1)

    def arrive(p, n):
        src, to = arrival(n)
        pre(p, src, to).wait_recv()
        pl.when(inside(to))(lambda: pre(p, src, to).start())
        pre_pair(p, src, c).start()

    def product(p):
        repeat(0, n_z, lambda src: pre_pair(p, src, 1 - c).wait_recv())

        def rows(i):
            row, col = chunk(i, width)
            term = jnp.dot(tok_t[row, :], pre_all[p, :, col], preferred_element_type=jnp.float32)
            out_part[p, i] = (term * scale).astype(jnp.bfloat16)

        repeat(0, n_dp, rows)
        repeat(1, n_dp, lambda j: rs(p, j).start())

    def own_sum(p):
        return pltpu.make_async_copy(sum_v.at[p], grad.at[place(p, d)], in_sem.at[4 + p])

    def reduce(p):
        repeat(1, n_dp, lambda j: rs(p, j).wait_recv())
        total = out_part[p, d].astype(jnp.float32)
        for j in range(1, n_dp):
            total = total + in_part[p, j].astype(jnp.float32)
        sum_v[p] = total.astype(jnp.bfloat16)
        repeat(1, n_dp, lambda j: ag(p, j, d).start())
        own_sum(p).start()

    last = n_z - 2
    for p in range(parts):
        if p == 0:
            repeat(0, last, lambda n: arrive(0, n))
            repeat(1, n_z, take_both)
        if p + 1 < parts:
            arrive(p + 1, 0)
        arrive(p, last)
        if p + 2 < parts:
            both_ways(lambda way: pre_own(p + 2, way), start)
            pre_pair(p + 2, z, c).start()
        if p + 1 < parts:
            repeat(1, last, lambda n: arrive(p + 1, n))
        product(p)
        if p > 0:
            reduce(p - 1)
    reduce(parts - 1)
    for p in range(parts):
        repeat(1, n_dp, lambda j: ag(p, j, (d - j + n_dp) % n_dp).wait_recv())
        own_sum(p).wait()

    hidden_out.wait()
    both_ways(f1_own, gone)
    sib_own().wait_send()
    tok(0, 1).wait_send()
    for p in range(parts):
        both_ways(lambda way: pre_own(p, way), gone)
        pre_pair(p, z, c).wait_send()
        repeat(1, n_dp, lambda j: rs(p, j).wait_send())
        repeat(1, n_dp, lambda j: ag(p, j, d).wait_send())

    def sent(n):
        src, to = arrival(n)
        pl.when(inside(to))(lambda: f1(src, to).wait_send())
        repeat(1, n_b, lambda j: piece(src, d, row_s, row_r, b_peer(j)).wait_send())
        repeat(1, n_a, lambda i: piece(src, d, col_s, col_r, a_peer(i)).wait_send())

        def corner(i):
            def corner_b(j):
                piece(src, b_peer(-j), d0_s, d0_r, a_peer(i), 0).wait_send()
                piece(src, a_peer(-i), d1_s, d1_r, b_peer(j), 1).wait_send()
            repeat(1, n_b, corner_b)
        repeat(1, n_a, corner)
        sib(src, c).wait_send()
        tok(n + 1, 0).wait_send()
        tok(n + 1, 1).wait_send()
        for p in range(parts):
            pl.when(inside(to))(lambda: pre(p, src, to).wait_send())
            pre_pair(p, src, c).wait_send()

    repeat(0, n_z - 1, sent)


def on_device(tokens, panel, cotangent):
    n_tok, depth_all = tokens.shape
    depth, cols = panel.shape
    n_tensor = lax.axis_size("tensor")
    n_dp = lax.axis_size("dp")
    n_z = n_tensor // 2
    scale = 1.0 / math.sqrt(n_tok * n_tensor * n_dp)
    chunk_rows = max(16, depth // n_dp)
    across = n_dp // (depth // chunk_rows)
    parts = max(p for p in (2, 4) if (cols // p // across) % LANES == 0)
    part = (parts, n_dp, chunk_rows, cols // parts // across)
    dma = pltpu.SemaphoreType.DMA
    anywhere = pl.BlockSpec(memory_space=pl.ANY)
    bf16, f32 = jnp.bfloat16, jnp.float32
    hidden, grad = pl.pallas_call(
        functools.partial(kernel, n_dp, n_tensor, parts, scale),
        out_shape=(
            jax.ShapeDtypeStruct((n_tok, cols // 2), f32),
            jax.ShapeDtypeStruct((depth, cols), bf16),
        ),
        in_specs=[anywhere] * 3,
        out_specs=(anywhere, anywhere),
        scratch_shapes=[
            pltpu.VMEM((n_tok, depth_all), bf16),
            pltpu.VMEM((n_tok, cols // 2), bf16),
            pltpu.VMEM((n_tok, cols // 2), f32),
            pltpu.VMEM((n_tensor, depth, cols), bf16),
            pltpu.VMEM((n_tensor, n_tok, depth), bf16),
            pltpu.VMEM((depth, n_tensor * n_tok), bf16),
            pltpu.VMEM((parts, n_tensor * n_tok, cols // parts), bf16),
            pltpu.VMEM((n_tok, cols), f32),
            pltpu.VMEM(part, bf16),
            pltpu.VMEM(part, bf16),
            pltpu.VMEM((parts,) + part[2:], bf16),
        ]
        + [dma((4 + parts,))]
        + [dma((n_z,))] * 12
        + [dma((parts, n_z))] * 4
        + [dma((2,)), dma((parts, 2))]
        + [dma((n_z, 2))] * 2
        + [dma((parts, n_dp))] * 4,
        compiler_params=pltpu.CompilerParams(
            collective_id=0, has_side_effects=True, vmem_limit_bytes=60 * 1024 * 1024
        ),
        cost_estimate=pl.CostEstimate(
            flops=4 * n_tok * depth_all * cols,
            bytes_accessed=4 * depth * cols,
            transcendentals=n_tok * cols // 2,
        ),
    )(tokens, panel, cotangent)
    return hidden, grad.astype(jnp.float32)


def solution(mesh):
    placed = (P(("dp", "tensor"), None), P("tensor", None), P(("dp", "tensor"), None))
    return jax.shard_map(
        on_device,
        mesh=mesh,
        in_specs=placed,
        out_specs=(P(("dp", "tensor"), None), P("tensor", None)),
        check_vma=False,
    )
```

```python
import functools
import math

import jax
import jax.numpy as jnp
from jax import lax
from jax.experimental import pallas as pl
from jax.experimental.pallas import tpu as pltpu
from jax.sharding import PartitionSpec as P

MESH = pl.DeviceIdType.MESH


def repeat(low, high, body):
    if high - low <= 4:
        for i in range(low, high):
            body(i)
    else:
        lax.fori_loop(low, high, lambda i, carry: (body(i), carry)[1], 0)


def factor(n):
    return max(f for f in range(1, math.isqrt(n) + 1) if n % f == 0)


def kernel(
    n_dp, n_tensor, parts, scale,
    tokens, panel, cotangent,
    hidden, grad,
    tok_v, ct_v, hid_v, full, tok_all, tok_t, pre_all, acc, out_part, in_part,
    in_sem, f1_s, f1_r, row_s, row_r, col_s, col_r, d0_s, d0_r, d1_s, d1_r, sib_s, sib_r,
    pair_s, pair_r, pre_s, pre_r, own_s, preo_s, tok_s, tok_r, rs_s, rs_r, ag_s, ag_r,
):
    n_tok, _ = tokens.shape
    depth, cols = panel.shape
    units = cols // 2
    width = cols // parts
    n_z = n_tensor // 2
    n_b = factor(n_dp)
    n_a = n_dp // n_b
    d, t = lax.axis_index("dp"), lax.axis_index("tensor")
    a, b = d // n_b, d % n_b
    z, c = t // 2, t % 2
    pair = z * 2 + 1 - c

    chunk_rows = max(16, depth // n_dp)
    down = depth // chunk_rows
    across = n_dp // down

    def chunk(i, span, half=None):
        wide = span // across
        row = pl.multiple_of((i // across) * chunk_rows, chunk_rows)
        start = (i % across) * wide
        if half is not None:
            wide = wide // 2
            start = start + half * wide
        return pl.ds(row, chunk_rows), pl.ds(pl.multiple_of(start, wide), wide)

    def send(src, dst, s, r, dp, tensor):
        return pltpu.make_async_remote_copy(
            src_ref=src, dst_ref=dst, send_sem=s, recv_sem=r,
            device_id=(dp, tensor), device_id_type=MESH,
        )

    def at_z(place, core):
        return place * 2 + core

    def arrival(n):
        short = jnp.minimum(z, n_z - 1 - z)
        both = n < 2 * short
        m = jnp.where(both, n // 2 + 1, n - short + 1)
        side = jnp.where(both, 2 * (n % 2) - 1, jnp.where(z > n_z - 1 - z, -1, 1))
        return z + side * m, z - side

    def inside(place):
        return (place >= 0) & (place < n_z)

    def f1_own(way):
        where = chunk(d, cols)
        to = at_z(z + 2 * way - 1, c)
        return send(panel.at[where], full.at[(t,) + where], own_s.at[way], f1_r.at[z], d, to)

    def f1(src, to):
        ref = full.at[(at_z(src, c),) + chunk(d, cols)]
        return send(ref, ref, f1_s.at[src], f1_r.at[src], d, at_z(to, c))

    def piece(src, i, s, r, to, half=None):
        ref = full.at[(at_z(src, c),) + chunk(i, cols, half)]
        return send(ref, ref, s.at[src], r.at[src], to, t)

    def a_peer(i):
        return ((a + i + n_a) % n_a) * n_b + b

    def b_peer(j):
        return a * n_b + (b + j + n_b) % n_b

    def ab_peer(i, j):
        return ((a + i + n_a) % n_a) * n_b + (b + j + n_b) % n_b

    def sib_own():
        return send(panel, full.at[t], sib_s.at[z], sib_r.at[z], d, pair)

    def sib(src, core):
        ref = full.at[at_z(src, core)]
        return send(ref, ref, sib_s.at[src], sib_r.at[src], d, pair)

    def far(k, core):
        return at_z((z + k + n_z) % n_z, core)

    def columns_of(i):
        return pl.ds(pl.multiple_of(i * depth, depth), depth)

    def rows_of(i):
        return pl.ds(pl.multiple_of(i * n_tok, n_tok), n_tok)

    def tok(k, other):
        to = far(k, (1 - c) if other else c)
        return send(
            tok_v.at[:, columns_of(to)], tok_all.at[t], tok_s.at[k, other], tok_r.at[k, other], d, to
        )

    def pre_own(p, way):
        ref = pre_all.at[p, rows_of(t)]
        to = at_z(z + 2 * way - 1, c)
        return send(ref, ref, preo_s.at[p, way], pre_r.at[p, z], d, to)

    def pre(p, src, to):
        ref = pre_all.at[p, rows_of(at_z(src, c))]
        return send(ref, ref, pre_s.at[p, src], pre_r.at[p, src], d, at_z(to, c))

    def pre_pair(p, src, core):
        ref = pre_all.at[p, rows_of(at_z(src, core))]
        return send(ref, ref, pair_s.at[p, src], pair_r.at[p, src], d, pair)

    def rs(p, j):
        to = (d + j) % n_dp
        return send(out_part.at[p, to], in_part.at[p, j], rs_s.at[p, j], rs_r.at[p, j], to, t)

    def place(p, i):
        row, col = chunk(i, width)
        return row, pl.ds(pl.multiple_of(p * width + col.start, col.size), col.size)

    def ag(p, j, i):
        ref = grad.at[place(p, i)]
        return send(ref, ref, ag_s.at[p, j], ag_r.at[p, j], (d + j) % n_dp, t)

    def both_ways(copy, act):
        pl.when(z > 0)(lambda: act(copy(0)))
        pl.when(z < n_z - 1)(lambda: act(copy(1)))

    def start(copy):
        copy.start()

    def gone(copy):
        copy.wait_send()

    tokens_in = pltpu.make_async_copy(tokens, tok_v, in_sem.at[0])
    panel_in = pltpu.make_async_copy(panel, full.at[t], in_sem.at[1])
    ct_in = pltpu.make_async_copy(cotangent, ct_v, in_sem.at[2])
    tokens_in.start()
    panel_in.start()
    ct_in.start()

    barrier = pltpu.get_barrier_semaphore()

    def greet_tensor(k):
        pl.semaphore_signal(barrier, inc=1, device_id=(d, (t + k) % n_tensor), device_id_type=MESH)

    def greet_dp(k):
        pl.semaphore_signal(barrier, inc=1, device_id=((d + k) % n_dp, t), device_id_type=MESH)

    repeat(1, n_tensor, greet_tensor)
    repeat(1, n_dp, greet_dp)
    pl.semaphore_wait(barrier, n_tensor + n_dp - 2)

    both_ways(f1_own, start)
    sib_own().start()
    tokens_in.wait()
    panel_in.wait()
    ct_in.wait()
    tok(0, 1).start()

    def multiply(own):
        return jnp.dot(tok_v[:, columns_of(own)], full[own], preferred_element_type=jnp.float32)

    acc[...] = multiply(t)

    def spread(n):
        src, to = arrival(n)
        f1(src, to).wait_recv()
        pl.when(inside(to))(lambda: f1(src, to).start())
        repeat(1, n_b, lambda j: piece(src, d, row_s, row_r, b_peer(j)).start())
        repeat(1, n_a, lambda i: piece(src, d, col_s, col_r, a_peer(i)).start())

    def exchange(k):
        tok(k, 0).start()
        tok(k, 1).start()

    def relay(n):
        src, _ = arrival(n)
        repeat(1, n_b, lambda j: piece(src, b_peer(-j), row_s, row_r, d).wait_recv())

        def pass_a(j):
            repeat(1, n_a, lambda i: piece(src, b_peer(-j), d0_s, d0_r, a_peer(i), 0).start())

        repeat(1, n_b, pass_a)
        repeat(1, n_a, lambda i: piece(src, a_peer(-i), col_s, col_r, d).wait_recv())

        def pass_b(i):
            repeat(1, n_b, lambda j: piece(src, a_peer(-i), d1_s, d1_r, b_peer(j), 1).start())

        repeat(1, n_a, pass_b)

    def finish(n):
        src, _ = arrival(n)

        def corner(i):
            def corner_b(j):
                piece(src, ab_peer(-i, -j), d0_s, d0_r, d, 0).wait_recv()
                piece(src, ab_peer(-i, -j), d1_s, d1_r, d, 1).wait_recv()
            repeat(1, n_b, corner_b)
        repeat(1, n_a, corner)
        sib(src, c).start()
        acc[...] += multiply(at_z(src, c))

    def other(src):
        sib(src, 1 - c).wait_recv()
        acc[...] += multiply(at_z(src, 1 - c))

    def when(n, body):
        if isinstance(n, int):
            if 0 <= n < n_z - 1:
                body(n)
        else:
            pl.when((n >= 0) & (n < n_z - 1))(lambda: body(n))

    def stage(n):
        when(n, spread)
        when(n - 1, relay)
        if isinstance(n, int):
            if n == n_z - 1:
                repeat(1, n_z, exchange)
        else:
            pl.when(n == n_z - 1)(lambda: repeat(1, n_z, exchange))
        when(n - 2, finish)
        when(n - 3, lambda m: other(arrival(m)[0]))

    stage(0)
    other(z)
    repeat(1, n_z + 2, stage)

    gate = acc[:, :units]
    up = acc[:, units:]
    s = jax.nn.sigmoid(gate)
    act = gate * s
    ct = ct_v[...].astype(jnp.float32)
    gate_grad = (ct * up * s * (1.0 + gate * (1.0 - s))).astype(jnp.bfloat16)
    up_grad = (ct * act).astype(jnp.bfloat16)
    for p in range(parts):
        term = gate_grad if p < parts // 2 else up_grad
        first = (p % (parts // 2)) * width
        pre_all[p, rows_of(t), :] = term[:, first:first + width]
        if p < 2:
            both_ways(lambda way: pre_own(p, way), start)
            pre_pair(p, z, c).start()
    hid_v[...] = act * up
    hidden_out = pltpu.make_async_copy(hid_v, hidden, in_sem.at[3])
    hidden_out.start()

    tok_t[:, rows_of(t)] = tok_v[:, columns_of(t)].T

    def take(own, k, index):
        dst = tok_all.at[own]
        send(dst, dst, tok_s.at[k, index], tok_r.at[k, index], d, pair).wait_recv()
        tok_t[:, rows_of(own)] = dst[...].T

    take(pair, 0, 1)

    def take_both(k):
        take(far(-k, c), k, 0)
        take(far(-k, 1 - c), k, 1)

    def arrive(p, n):
        src, to = arrival(n)
        pre(p, src, to).wait_recv()
        pl.when(inside(to))(lambda: pre(p, src, to).start())
        pre_pair(p, src, c).start()

    def product(p):
        repeat(0, n_z, lambda src: pre_pair(p, src, 1 - c).wait_recv())

        def rows(i):
            row, col = chunk(i, width)
            term = jnp.dot(tok_t[row, :], pre_all[p, :, col], preferred_element_type=jnp.float32)
            out_part[p, i] = (term * scale).astype(jnp.bfloat16)

        repeat(0, n_dp, rows)
        repeat(1, n_dp, lambda j: rs(p, j).start())

    def reduce(p):
        repeat(1, n_dp, lambda j: rs(p, j).wait_recv())
        total = out_part[p, d].astype(jnp.float32)
        for j in range(1, n_dp):
            total = total + in_part[p, j].astype(jnp.float32)
        grad[place(p, d)] = total.astype(jnp.bfloat16)
        repeat(1, n_dp, lambda j: ag(p, j, d).start())

    last = n_z - 2
    for p in range(parts):
        if p == 0:
            repeat(0, last, lambda n: arrive(0, n))
            repeat(1, n_z, take_both)
        if p + 1 < parts:
            arrive(p + 1, 0)
        arrive(p, last)
        if p + 2 < parts:
            both_ways(lambda way: pre_own(p + 2, way), start)
            pre_pair(p + 2, z, c).start()
        if p + 1 < parts:
            repeat(1, last, lambda n: arrive(p + 1, n))
        product(p)
        if p > 0:
            reduce(p - 1)
    reduce(parts - 1)
    for p in range(parts):
        repeat(1, n_dp, lambda j: ag(p, j, (d - j + n_dp) % n_dp).wait_recv())

    hidden_out.wait()
    both_ways(f1_own, gone)
    sib_own().wait_send()
    tok(0, 1).wait_send()
    for p in range(parts):
        both_ways(lambda way: pre_own(p, way), gone)
        pre_pair(p, z, c).wait_send()
        repeat(1, n_dp, lambda j: rs(p, j).wait_send())
        repeat(1, n_dp, lambda j: ag(p, j, d).wait_send())

    def sent(n):
        src, to = arrival(n)
        pl.when(inside(to))(lambda: f1(src, to).wait_send())
        repeat(1, n_b, lambda j: piece(src, d, row_s, row_r, b_peer(j)).wait_send())
        repeat(1, n_a, lambda i: piece(src, d, col_s, col_r, a_peer(i)).wait_send())

        def corner(i):
            def corner_b(j):
                piece(src, b_peer(-j), d0_s, d0_r, a_peer(i), 0).wait_send()
                piece(src, a_peer(-i), d1_s, d1_r, b_peer(j), 1).wait_send()
            repeat(1, n_b, corner_b)
        repeat(1, n_a, corner)
        sib(src, c).wait_send()
        tok(n + 1, 0).wait_send()
        tok(n + 1, 1).wait_send()
        for p in range(parts):
            pl.when(inside(to))(lambda: pre(p, src, to).wait_send())
            pre_pair(p, src, c).wait_send()

    repeat(0, n_z - 1, sent)


def on_device(tokens, panel, cotangent):
    n_tok, depth_all = tokens.shape
    depth, cols = panel.shape
    n_tensor = lax.axis_size("tensor")
    n_dp = lax.axis_size("dp")
    n_z = n_tensor // 2
    scale = 1.0 / math.sqrt(n_tok * n_tensor * n_dp)
    chunk_rows = max(16, depth // n_dp)
    across = n_dp // (depth // chunk_rows)
    parts = 2
    part = (parts, n_dp, chunk_rows, cols // parts // across)
    dma = pltpu.SemaphoreType.DMA
    anywhere = pl.BlockSpec(memory_space=pl.ANY)
    bf16, f32 = jnp.bfloat16, jnp.float32
    hidden, grad = pl.pallas_call(
        functools.partial(kernel, n_dp, n_tensor, parts, scale),
        out_shape=(
            jax.ShapeDtypeStruct((n_tok, cols // 2), f32),
            jax.ShapeDtypeStruct((depth, cols), bf16),
        ),
        in_specs=[anywhere] * 3,
        out_specs=(anywhere, pl.BlockSpec(memory_space=pltpu.VMEM)),
        scratch_shapes=[
            pltpu.VMEM((n_tok, depth_all), bf16),
            pltpu.VMEM((n_tok, cols // 2), bf16),
            pltpu.VMEM((n_tok, cols // 2), f32),
            pltpu.VMEM((n_tensor, depth, cols), bf16),
            pltpu.VMEM((n_tensor, n_tok, depth), bf16),
            pltpu.VMEM((depth, n_tensor * n_tok), bf16),
            pltpu.VMEM((parts, n_tensor * n_tok, cols // parts), bf16),
            pltpu.VMEM((n_tok, cols), f32),
            pltpu.VMEM(part, bf16),
            pltpu.VMEM(part, bf16),
        ]
        + [dma((4,))]
        + [dma((n_z,))] * 12
        + [dma((parts, n_z))] * 4
        + [dma((2,)), dma((parts, 2))]
        + [dma((n_z, 2))] * 2
        + [dma((parts, n_dp))] * 4,
        compiler_params=pltpu.CompilerParams(
            collective_id=0, has_side_effects=True, vmem_limit_bytes=60 * 1024 * 1024
        ),
        cost_estimate=pl.CostEstimate(
            flops=4 * n_tok * depth_all * cols,
            bytes_accessed=4 * depth * cols,
            transcendentals=n_tok * cols // 2,
        ),
    )(tokens, panel, cotangent)
    return hidden, grad.astype(jnp.float32)


def solution(mesh):
    placed = (P(("dp", "tensor"), None), P("tensor", None), P(("dp", "tensor"), None))
    return jax.shard_map(
        on_device,
        mesh=mesh,
        in_specs=placed,
        out_specs=(P(("dp", "tensor"), None), P("tensor", None)),
        check_vma=False,
    )
```

```python
import functools
import math

import jax
import jax.numpy as jnp
from jax import lax
from jax.experimental import pallas as pl
from jax.experimental.pallas import tpu as pltpu
from jax.sharding import PartitionSpec as P

MESH = pl.DeviceIdType.MESH
PARTS = 2
LANES = 128


def repeat(low, high, body):
    if high - low <= 4:
        for i in range(low, high):
            body(i)
    else:
        lax.fori_loop(low, high, lambda i, carry: (body(i), carry)[1], 0)


def team_size(n_dp, depth):
    return max(s for s in range(1, n_dp + 1) if n_dp % s == 0 and depth % (s * LANES) == 0)


def kernel(
    n_dp, n_tensor, n_s, scale,
    tokens, panel, cotangent,
    hidden, grad,
    tok_v, ct_v, hid_v, stage, tok_x, tok_t, pan, mate_out, mate_in, sum_out, sum_in, own_part,
    proj, pre_all, row_own, row_out, row_in, team_in,
    in_sem, own_s, pan_s, pan_r, tok_s, tok_r, mate_s, mate_r, sum_s, sum_r,
    pre_s, pre_r, pair_s, pair_r, row_s, row_r, team_s, team_r, ag_s, ag_r,
):
    n_tok, _ = tokens.shape
    depth, cols = panel.shape
    width = cols // PARTS
    n_z = n_tensor // 2
    n_g = n_dp // n_s
    r = depth // n_s
    d, t = lax.axis_index("dp"), lax.axis_index("tensor")
    g, s = d // n_s, d % n_s
    z, c = t // 2, t % 2
    pair = z * 2 + 1 - c

    def send(src, dst, s_sem, r_sem, dp, tensor):
        return pltpu.make_async_remote_copy(
            src_ref=src, dst_ref=dst, send_sem=s_sem, recv_sem=r_sem,
            device_id=(dp, tensor), device_id_type=MESH,
        )

    def arrival(n):
        short = jnp.minimum(z, n_z - 1 - z)
        both = n < 2 * short
        m = jnp.where(both, n // 2 + 1, n - short + 1)
        side = jnp.where(both, 2 * (n % 2) - 1, jnp.where(z > n_z - 1 - z, -1, 1))
        return z + side * m, z - side

    def inside(place):
        return (place >= 0) & (place < n_z)

    def slots(i, size):
        return pl.ds(pl.multiple_of(i * size, size), size)

    def mate(j):
        return (s + j) % n_s

    def dp_of(i):
        return g * n_s + i

    def part(p):
        return pl.ds(p * width, width)

    def pan_own(way):
        to = (z + 2 * way - 1) * 2 + c
        return send(panel.at[slots(s, r)], pan.at[slots(z, r)], own_s.at[way], pan_r.at[z], d, to)

    def pan_on(src, to):
        ref = pan.at[slots(src, r)]
        return send(ref, ref, pan_s.at[src], pan_r.at[src], d, to * 2 + c)

    my_slot = c * n_s + s

    def tok(k):
        e = (my_slot + k) % (2 * n_s)
        return send(
            stage.at[e], tok_x.at[slots(my_slot, n_tok)], tok_s.at[k], tok_r.at[k],
            dp_of(e % n_s), z * 2 + e // n_s,
        )

    def halfway(p):
        return send(mate_out.at[p], mate_in.at[p], mate_s.at[p], mate_r.at[p], d, pair)

    def sums(p, j):
        to = mate(j)
        return send(
            sum_out.at[p, slots(to, n_tok)], sum_in.at[p, j], sum_s.at[p, j], sum_r.at[p, j], dp_of(to), t
        )

    def pre(p, j, owner):
        ref = pre_all.at[p, slots(c * n_s + owner, n_tok)]
        return send(ref, ref, pre_s.at[p, j], pre_r.at[p, j], dp_of(mate(j)), t)

    def pre_pair(p, j, core):
        ref = pre_all.at[p, slots(core * n_s + mate(-j + n_s), n_tok)]
        return send(ref, ref, pair_s.at[p, j], pair_r.at[p, j], d, pair)

    def rows_to(p, k):
        to = (z + k) % n_z
        return send(
            row_out.at[p, slots(to, r)], row_in.at[p, k], row_s.at[p, k], row_r.at[p, k], d, to * 2 + c
        )

    def team(p, k):
        return send(
            team_in.at[p, g], team_in.at[p, g], team_s.at[p, k], team_r.at[p, k],
            ((g + k) % n_g) * n_s + s, t,
        )

    def ag(p, j, owner):
        ref = grad.at[slots(owner, r), part(p)]
        return send(ref, ref, ag_s.at[p, j], ag_r.at[p, j], dp_of(mate(j)), t)

    def both_ways(copy, act):
        pl.when(z > 0)(lambda: act(copy(0)))
        pl.when(z < n_z - 1)(lambda: act(copy(1)))

    tokens_in = pltpu.make_async_copy(tokens, tok_v, in_sem.at[0])
    panel_in = pltpu.make_async_copy(panel.at[slots(s, r)], pan.at[slots(z, r)], in_sem.at[1])
    ct_in = pltpu.make_async_copy(cotangent, ct_v, in_sem.at[2])
    tokens_in.start()
    panel_in.start()
    ct_in.start()

    barrier = pltpu.get_barrier_semaphore()

    def greet(dp, tensor):
        pl.semaphore_signal(barrier, inc=1, device_id=(dp, tensor), device_id_type=MESH)

    def greet_plane(k):
        e = (my_slot + k) % (2 * n_s)
        greet(dp_of(e % n_s), z * 2 + e // n_s)

    repeat(1, n_z, lambda k: greet(d, ((z + k) % n_z) * 2 + c))
    repeat(1, 2 * n_s, greet_plane)
    repeat(1, n_g, lambda k: greet(((g + k) % n_g) * n_s + s, t))
    pl.semaphore_wait(barrier, n_z + 2 * n_s + n_g - 3)

    both_ways(pan_own, lambda copy: copy.start())
    tokens_in.wait()

    for e in range(2 * n_s):
        for i in range(n_z):
            first = (i * 2 + e // n_s) * depth + (e % n_s) * r
            stage[e, :, i * r:(i + 1) * r] = tok_v[:, first:first + r]
    repeat(1, 2 * n_s, lambda k: tok(k).start())
    tok_x[slots(my_slot, n_tok), :] = stage[my_slot]
    tok_t[:, slots(my_slot, n_tok)] = stage[my_slot].T

    def pass_on(n):
        src, to = arrival(n)
        pan_on(src, to).wait_recv()
        pl.when(inside(to))(lambda: pan_on(src, to).start())

    def take(k):
        e = (my_slot - k + 2 * n_s) % (2 * n_s)
        ref = tok_x.at[slots(e, n_tok)]
        send(ref, ref, tok_s.at[k], tok_r.at[k], d, pair).wait_recv()
        tok_t[:, slots(e, n_tok)] = ref[...].T

    if n_z > 1:
        pass_on(0)
    repeat(1, n_s, take)
    repeat(1, n_z - 2, pass_on)
    repeat(n_s, 2 * n_s, take)
    if n_z > 2:
        pass_on(n_z - 2)
    panel_in.wait()
    ct_in.wait()

    team_rows = n_s * n_tok
    for p in range(PARTS):
        mate_out[p] = jnp.dot(
            tok_x[slots(1 - c, team_rows), :], pan[:, part(p)], preferred_element_type=jnp.float32
        ).astype(jnp.bfloat16)
        halfway(p).start()
    for p in range(PARTS):
        own_part[...] = jnp.dot(
            tok_x[slots(c, team_rows), :], pan[:, part(p)], preferred_element_type=jnp.float32
        )
        halfway(p).wait_recv()
        own_part[...] += mate_in[p].astype(jnp.float32)
        sum_out[p] = own_part[...].astype(jnp.bfloat16)
        repeat(1, n_s, lambda j: sums(p, j).start())
        proj[:, part(p)] = own_part[slots(s, n_tok), :]
    for p in range(PARTS):
        def add(j):
            sums(p, j).wait_recv()
            proj[:, part(p)] += sum_in[p, j].astype(jnp.float32)

        repeat(1, n_s, add)

    gate = proj[:, part(0)]
    up = proj[:, part(1)]
    sig = jax.nn.sigmoid(gate)
    act = gate * sig
    ct = ct_v[...].astype(jnp.float32)
    pre_all[0, slots(my_slot, n_tok), :] = (ct * up * sig * (1.0 + gate * (1.0 - sig))).astype(jnp.bfloat16)
    pre_all[1, slots(my_slot, n_tok), :] = (ct * act).astype(jnp.bfloat16)
    for p in range(PARTS):
        repeat(1, n_s, lambda j: pre(p, j, s).start())
        pre_pair(p, 0, c).start()
    hid_v[...] = act * up
    hidden_out = pltpu.make_async_copy(hid_v, hidden, in_sem.at[3])
    hidden_out.start()

    def finish(p):
        own_rows = row_own.at[p]

        def add(k):
            rows_to(p, k).wait_recv()
            own_rows[...] += row_in[p, k].astype(jnp.float32)

        repeat(1, n_z, add)
        if n_g > 1:
            team_in[p, g] = own_rows[...].astype(jnp.bfloat16)
            repeat(1, n_g, lambda k: team(p, k).start())

            def others(k):
                ref = team_in.at[p, (g - k + n_g) % n_g]
                send(ref, ref, team_s.at[p, k], team_r.at[p, k], d, pair).wait_recv()

            repeat(1, n_g, others)
            own_rows[...] = jnp.zeros((r, width), jnp.float32)

            def add_team(i):
                own_rows[...] += team_in[p, i].astype(jnp.float32)

            repeat(0, n_g, add_team)
        grad[slots(s, r), part(p)] = own_rows[...].astype(jnp.bfloat16)
        repeat(1, n_s, lambda j: ag(p, j, s).start())

    for p in range(PARTS):
        def arrive(j):
            pre(p, j, mate(-j + n_s)).wait_recv()
            pre_pair(p, j, c).start()

        repeat(1, n_s, arrive)
        repeat(0, n_s, lambda j: pre_pair(p, j, 1 - c).wait_recv())

        def product(k):
            to = (z + k) % n_z
            return scale * jnp.dot(
                tok_t[slots(to, r), :], pre_all[p], preferred_element_type=jnp.float32
            )

        def product_out(k):
            row_out[p, slots((z + k) % n_z, r), :] = product(k).astype(jnp.bfloat16)
            rows_to(p, k).start()

        repeat(1, n_z, product_out)
        row_own[p] = product(0)
    for p in range(PARTS):
        finish(p)
    for p in range(PARTS):
        repeat(1, n_s, lambda j: ag(p, j, mate(-j + n_s)).wait_recv())

    hidden_out.wait()
    both_ways(pan_own, lambda copy: copy.wait_send())

    def passed_on(n):
        src, to = arrival(n)
        pl.when(inside(to))(lambda: pan_on(src, to).wait_send())

    repeat(0, n_z - 1, passed_on)
    repeat(1, 2 * n_s, lambda k: tok(k).wait_send())
    for p in range(PARTS):
        halfway(p).wait_send()
        repeat(1, n_z, lambda k: rows_to(p, k).wait_send())
        repeat(1, n_g, lambda k: team(p, k).wait_send())
        repeat(0, n_s, lambda j: pre_pair(p, j, c).wait_send())

        def sent(j):
            sums(p, j).wait_send()
            pre(p, j, s).wait_send()
            ag(p, j, s).wait_send()

        repeat(1, n_s, sent)


def on_device(tokens, panel, cotangent):
    n_tok, depth_all = tokens.shape
    depth, cols = panel.shape
    n_tensor = lax.axis_size("tensor")
    n_dp = lax.axis_size("dp")
    n_z = n_tensor // 2
    n_s = team_size(n_dp, depth)
    n_g = n_dp // n_s
    r = depth // n_s
    scale = 1.0 / math.sqrt(n_tok * n_tensor * n_dp)
    width = cols // PARTS
    team = n_s * n_tok
    dma = pltpu.SemaphoreType.DMA
    anywhere = pl.BlockSpec(memory_space=pl.ANY)
    bf16, f32 = jnp.bfloat16, jnp.float32
    hidden, grad = pl.pallas_call(
        functools.partial(kernel, n_dp, n_tensor, n_s, scale),
        out_shape=(
            jax.ShapeDtypeStruct((n_tok, cols // 2), f32),
            jax.ShapeDtypeStruct((depth, cols), bf16),
        ),
        in_specs=[anywhere] * 3,
        out_specs=(anywhere, pl.BlockSpec(memory_space=pltpu.VMEM)),
        scratch_shapes=[
            pltpu.VMEM((n_tok, depth_all), bf16),
            pltpu.VMEM((n_tok, cols // 2), bf16),
            pltpu.VMEM((n_tok, cols // 2), f32),
            pltpu.VMEM((2 * n_s, n_tok, n_z * r), bf16),
            pltpu.VMEM((2 * team, n_z * r), bf16),
            pltpu.VMEM((n_z * r, 2 * team), bf16),
            pltpu.VMEM((n_z * r, cols), bf16),
            pltpu.VMEM((PARTS, team, width), bf16),
            pltpu.VMEM((PARTS, team, width), bf16),
            pltpu.VMEM((PARTS, team, width), bf16),
            pltpu.VMEM((PARTS, n_s, n_tok, width), bf16),
            pltpu.VMEM((team, width), f32),
            pltpu.VMEM((n_tok, cols), f32),
            pltpu.VMEM((PARTS, 2 * team, width), bf16),
            pltpu.VMEM((PARTS, r, width), f32),
            pltpu.VMEM((PARTS, n_z * r, width), bf16),
            pltpu.VMEM((PARTS, n_z, r, width), bf16),
            pltpu.VMEM((PARTS, n_g, r, width), bf16),
        ]
        + [dma((4,)), dma((2,)), dma((n_z,)), dma((n_z,)), dma((2 * n_s,)), dma((2 * n_s,))]
        + [dma((PARTS,))] * 2
        + [dma((PARTS, n_s))] * 6
        + [dma((PARTS, n_z))] * 2
        + [dma((PARTS, n_g))] * 2
        + [dma((PARTS, n_s))] * 2,
        compiler_params=pltpu.CompilerParams(
            collective_id=0, has_side_effects=True, vmem_limit_bytes=60 * 1024 * 1024
        ),
        cost_estimate=pl.CostEstimate(
            flops=4 * n_tok * depth_all * cols,
            bytes_accessed=4 * depth * cols,
            transcendentals=n_tok * cols // 2,
        ),
    )(tokens, panel, cotangent)
    return hidden, grad.astype(jnp.float32)


def solution(mesh):
    placed = (P(("dp", "tensor"), None), P("tensor", None), P(("dp", "tensor"), None))
    return jax.shard_map(
        on_device,
        mesh=mesh,
        in_specs=placed,
        out_specs=(P(("dp", "tensor"), None), P("tensor", None)),
        check_vma=False,
    )
```

```python
import functools
import math

import jax
import jax.numpy as jnp
from jax import lax
from jax.experimental import pallas as pl
from jax.experimental.pallas import tpu as pltpu
from jax.sharding import PartitionSpec as P

MESH = pl.DeviceIdType.MESH
PARTS = 2
LANES = 128


def repeat(low, high, body):
    if high - low <= 4:
        for i in range(low, high):
            body(i)
    else:
        lax.fori_loop(low, high, lambda i, carry: (body(i), carry)[1], 0)


def team_size(n_dp, depth):
    return max(s for s in range(1, n_dp + 1) if n_dp % s == 0 and depth % (s * LANES) == 0)


def kernel(
    n_dp, n_tensor, n_s, scale,
    tokens, panel, cotangent,
    hidden, grad,
    tok_v, ct_v, hid_v, stage, tok_x, tok_t, pan, mate_out, mate_in, sum_out, sum_in, own_part,
    proj, pre_all, row_own, row_out, row_in, team_in,
    in_sem, pan_sem, own_s, pan_s, pan_r, tok_s, tok_r, mate_s, mate_r, sum_s, sum_r,
    pre_s, pre_r, pair_s, pair_r, row_s, row_r, team_s, team_r, ag_s, ag_r,
):
    n_tok, _ = tokens.shape
    depth, cols = panel.shape
    width = cols // PARTS
    n_z = n_tensor // 2
    n_g = n_dp // n_s
    r = depth // n_s
    d, t = lax.axis_index("dp"), lax.axis_index("tensor")
    g, s = d // n_s, d % n_s
    z, c = t // 2, t % 2
    pair = z * 2 + 1 - c

    def send(src, dst, s_sem, r_sem, dp, tensor):
        return pltpu.make_async_remote_copy(
            src_ref=src, dst_ref=dst, send_sem=s_sem, recv_sem=r_sem,
            device_id=(dp, tensor), device_id_type=MESH,
        )

    def arrival(n):
        short = jnp.minimum(z, n_z - 1 - z)
        both = n < 2 * short
        m = jnp.where(both, n // 2 + 1, n - short + 1)
        side = jnp.where(both, 2 * (n % 2) - 1, jnp.where(z > n_z - 1 - z, -1, 1))
        return z + side * m, z - side

    def inside(place):
        return (place >= 0) & (place < n_z)

    def slots(i, size):
        return pl.ds(pl.multiple_of(i * size, size), size)

    def mate(j):
        return (s + j) % n_s

    def dp_of(i):
        return g * n_s + i

    units = cols // 2
    half = width // 2

    def columns(p, up):
        return pl.ds(up * units + p * half, half)

    def pan_in(p, up):
        return pltpu.make_async_copy(
            panel.at[slots(s, r), columns(p, up)],
            pan.at[p, slots(z, r), pl.ds(up * half, half)],
            pan_sem.at[p, up],
        )

    def pan_own(p, way):
        ref = pan.at[p, slots(z, r)]
        to = (z + 2 * way - 1) * 2 + c
        return send(ref, ref, own_s.at[p, way], pan_r.at[p, z], d, to)

    def pan_on(p, src, to):
        ref = pan.at[p, slots(src, r)]
        return send(ref, ref, pan_s.at[p, src], pan_r.at[p, src], d, to * 2 + c)

    my_slot = c * n_s + s

    def tok(k):
        e = (my_slot + k) % (2 * n_s)
        return send(
            stage.at[e], tok_x.at[slots(my_slot, n_tok)], tok_s.at[k], tok_r.at[k],
            dp_of(e % n_s), z * 2 + e // n_s,
        )

    def halfway(p):
        return send(mate_out.at[p], mate_in.at[p], mate_s.at[p], mate_r.at[p], d, pair)

    def sums(p, j):
        to = mate(j)
        return send(
            sum_out.at[p, slots(to, n_tok)], sum_in.at[p, j], sum_s.at[p, j], sum_r.at[p, j], dp_of(to), t
        )

    def pre(p, j, owner):
        ref = pre_all.at[p, slots(c * n_s + owner, n_tok)]
        return send(ref, ref, pre_s.at[p, j], pre_r.at[p, j], dp_of(mate(j)), t)

    def pre_pair(p, j, core):
        ref = pre_all.at[p, slots(core * n_s + mate(-j + n_s), n_tok)]
        return send(ref, ref, pair_s.at[p, j], pair_r.at[p, j], d, pair)

    def rows_to(p, k):
        to = (z + k) % n_z
        return send(
            row_out.at[p, slots(to, r)], row_in.at[p, k], row_s.at[p, k], row_r.at[p, k], d, to * 2 + c
        )

    def team(p, k):
        return send(
            team_in.at[p, g], team_in.at[p, g], team_s.at[p, k], team_r.at[p, k],
            ((g + k) % n_g) * n_s + s, t,
        )

    def ag(p, j, owner, up):
        ref = grad.at[slots(owner, r), columns(p, up)]
        return send(ref, ref, ag_s.at[p, j, up], ag_r.at[p, j, up], dp_of(mate(j)), t)

    def both_ways(copy, act):
        pl.when(z > 0)(lambda: act(copy(0)))
        pl.when(z < n_z - 1)(lambda: act(copy(1)))

    for p in range(PARTS):
        pan_in(p, 0).start()
        pan_in(p, 1).start()
    tokens_in = pltpu.make_async_copy(tokens, tok_v, in_sem.at[0])
    ct_in = pltpu.make_async_copy(cotangent, ct_v, in_sem.at[1])
    tokens_in.start()
    ct_in.start()

    barrier = pltpu.get_barrier_semaphore()

    def greet(dp, tensor):
        pl.semaphore_signal(barrier, inc=1, device_id=(dp, tensor), device_id_type=MESH)

    def greet_plane(k):
        e = (my_slot + k) % (2 * n_s)
        greet(dp_of(e % n_s), z * 2 + e // n_s)

    repeat(1, n_z, lambda k: greet(d, ((z + k) % n_z) * 2 + c))
    repeat(1, 2 * n_s, greet_plane)
    repeat(1, n_g, lambda k: greet(((g + k) % n_g) * n_s + s, t))
    pl.semaphore_wait(barrier, n_z + 2 * n_s + n_g - 3)

    def offer(p):
        pan_in(p, 0).wait()
        pan_in(p, 1).wait()
        both_ways(lambda way: pan_own(p, way), lambda copy: copy.start())

    offer(0)
    tokens_in.wait()

    for e in range(2 * n_s):
        for i in range(n_z):
            first = (i * 2 + e // n_s) * depth + (e % n_s) * r
            stage[e, :, i * r:(i + 1) * r] = tok_v[:, first:first + r]
    repeat(1, 2 * n_s, lambda k: tok(k).start())
    tok_x[slots(my_slot, n_tok), :] = stage[my_slot]
    ct_in.wait()

    def pass_on(p, n):
        src, to = arrival(n)
        pan_on(p, src, to).wait_recv()
        pl.when(inside(to))(lambda: pan_on(p, src, to).start())

    def take(k):
        ref = tok_x.at[slots((my_slot - k + 2 * n_s) % (2 * n_s), n_tok)]
        send(ref, ref, tok_s.at[k], tok_r.at[k], d, pair).wait_recv()

    def transpose(e):
        tok_t[:, slots(e, n_tok)] = tok_x[slots(e, n_tok), :].T

    team_rows = n_s * n_tok

    def partial(p):
        mate_out[p] = jnp.dot(
            tok_x[slots(1 - c, team_rows), :], pan[p], preferred_element_type=jnp.float32
        ).astype(jnp.bfloat16)
        halfway(p).start()
        own_part[...] = jnp.dot(
            tok_x[slots(c, team_rows), :], pan[p], preferred_element_type=jnp.float32
        )
        halfway(p).wait_recv()
        own_part[...] += mate_in[p].astype(jnp.float32)
        sum_out[p] = own_part[...].astype(jnp.bfloat16)
        repeat(1, n_s, lambda j: sums(p, j).start())
        proj[p] = own_part[slots(s, n_tok), :]

    def activate(p):
        def add(j):
            sums(p, j).wait_recv()
            proj[p] += sum_in[p, j].astype(jnp.float32)

        repeat(1, n_s, add)
        gate = proj[p, :, :half]
        up = proj[p, :, half:]
        sig = jax.nn.sigmoid(gate)
        act = gate * sig
        ct = ct_v[:, p * half:(p + 1) * half].astype(jnp.float32)
        gate_grad = ct * up * sig * (1.0 + gate * (1.0 - sig))
        pre_all[p, slots(my_slot, n_tok), :half] = gate_grad.astype(jnp.bfloat16)
        pre_all[p, slots(my_slot, n_tok), half:] = (ct * act).astype(jnp.bfloat16)
        repeat(1, n_s, lambda j: pre(p, j, s).start())
        pre_pair(p, 0, c).start()
        hid_v[:, p * half:(p + 1) * half] = act * up

    def gather(p):
        def arrive(j):
            pre(p, j, mate(-j + n_s)).wait_recv()
            pre_pair(p, j, c).start()

        repeat(1, n_s, arrive)

    def product(p, k):
        to = (z + k) % n_z
        return scale * jnp.dot(
            tok_t[slots(to, r), :], pre_all[p], preferred_element_type=jnp.float32
        )

    def rows_out(p):
        repeat(0, n_s, lambda j: pre_pair(p, j, 1 - c).wait_recv())

        def product_out(k):
            row_out[p, slots((z + k) % n_z, r), :] = product(p, k).astype(jnp.bfloat16)
            rows_to(p, k).start()

        repeat(1, n_z, product_out)
        row_own[p] = product(p, 0)

    def finish(p):
        own_rows = row_own.at[p]

        def add(k):
            rows_to(p, k).wait_recv()
            own_rows[...] += row_in[p, k].astype(jnp.float32)

        repeat(1, n_z, add)
        if n_g > 1:
            team_in[p, g] = own_rows[...].astype(jnp.bfloat16)
            repeat(1, n_g, lambda k: team(p, k).start())

            def others(k):
                ref = team_in.at[p, (g - k + n_g) % n_g]
                send(ref, ref, team_s.at[p, k], team_r.at[p, k], d, pair).wait_recv()

            repeat(1, n_g, others)
            own_rows[...] = jnp.zeros((r, width), jnp.float32)

            def add_team(i):
                own_rows[...] += team_in[p, i].astype(jnp.float32)

            repeat(0, n_g, add_team)
        for up in range(2):
            grad[slots(s, r), columns(p, up)] = own_rows[:, up * half:(up + 1) * half].astype(jnp.bfloat16)
            repeat(1, n_s, lambda j: ag(p, j, s, up).start())

    hidden_out = pltpu.make_async_copy(hid_v, hidden, in_sem.at[2])

    z_time, xy_time, sum_time = 16.0 / PARTS, 10.5 / PARTS, 21.0 / PARTS
    plan = []
    for p in range(PARTS):
        for n in range(n_z - 1):
            plan.append((z_time * (p + (n + 1) / (n_z - 1)) + 1.0 + n / n_z, functools.partial(pass_on, p, n)))
            if n == 0 and p + 1 < PARTS:
                plan.append((plan[-1][0] + 0.01, functools.partial(offer, p + 1)))
        ready = z_time * (p + 1) + 2.0
        plan.append((ready, functools.partial(partial, p)))
        ready = max(ready + 3.0, 13.0 + xy_time * p) + xy_time
        plan.append((ready, functools.partial(activate, p)))
        ready = ready + 1.5 + xy_time
        plan.append((ready, functools.partial(gather, p)))
        ready = ready + 1.0
        plan.append((ready, functools.partial(rows_out, p)))
        ready = max(ready + 1.5, 27.0 + sum_time * p) + sum_time
        plan.append((ready, functools.partial(finish, p)))
    last_partial = z_time * PARTS + 2.0
    plan.append((z_time + 1.99, lambda: repeat(1, 2 * n_s, take)))
    plan.append((last_partial + 0.01, lambda: repeat(0, 2 * n_s, transpose)))
    for _, run in sorted(plan, key=lambda item: item[0]):
        run()
    hidden_out.start()
    for p in range(PARTS):
        for up in range(2):
            repeat(1, n_s, lambda j: ag(p, j, mate(-j + n_s), up).wait_recv())

    hidden_out.wait()
    repeat(1, 2 * n_s, lambda k: tok(k).wait_send())
    for p in range(PARTS):
        both_ways(lambda way: pan_own(p, way), lambda copy: copy.wait_send())

        def passed_on(n):
            src, to = arrival(n)
            pl.when(inside(to))(lambda: pan_on(p, src, to).wait_send())

        repeat(0, n_z - 1, passed_on)
        halfway(p).wait_send()
        repeat(1, n_z, lambda k: rows_to(p, k).wait_send())
        repeat(1, n_g, lambda k: team(p, k).wait_send())
        repeat(0, n_s, lambda j: pre_pair(p, j, c).wait_send())

        def sent(j):
            sums(p, j).wait_send()
            pre(p, j, s).wait_send()
            ag(p, j, s, 0).wait_send()
            ag(p, j, s, 1).wait_send()

        repeat(1, n_s, sent)


def on_device(tokens, panel, cotangent):
    n_tok, depth_all = tokens.shape
    depth, cols = panel.shape
    n_tensor = lax.axis_size("tensor")
    n_dp = lax.axis_size("dp")
    n_z = n_tensor // 2
    n_s = team_size(n_dp, depth)
    n_g = n_dp // n_s
    r = depth // n_s
    scale = 1.0 / math.sqrt(n_tok * n_tensor * n_dp)
    width = cols // PARTS
    team = n_s * n_tok
    dma = pltpu.SemaphoreType.DMA
    anywhere = pl.BlockSpec(memory_space=pl.ANY)
    bf16, f32 = jnp.bfloat16, jnp.float32
    hidden, grad = pl.pallas_call(
        functools.partial(kernel, n_dp, n_tensor, n_s, scale),
        out_shape=(
            jax.ShapeDtypeStruct((n_tok, cols // 2), f32),
            jax.ShapeDtypeStruct((depth, cols), bf16),
        ),
        in_specs=[anywhere] * 3,
        out_specs=(anywhere, pl.BlockSpec(memory_space=pltpu.VMEM)),
        scratch_shapes=[
            pltpu.VMEM((n_tok, depth_all), bf16),
            pltpu.VMEM((n_tok, cols // 2), bf16),
            pltpu.VMEM((n_tok, cols // 2), f32),
            pltpu.VMEM((2 * n_s, n_tok, n_z * r), bf16),
            pltpu.VMEM((2 * team, n_z * r), bf16),
            pltpu.VMEM((n_z * r, 2 * team), bf16),
            pltpu.VMEM((PARTS, n_z * r, width), bf16),
            pltpu.VMEM((PARTS, team, width), bf16),
            pltpu.VMEM((PARTS, team, width), bf16),
            pltpu.VMEM((PARTS, team, width), bf16),
            pltpu.VMEM((PARTS, n_s, n_tok, width), bf16),
            pltpu.VMEM((team, width), f32),
            pltpu.VMEM((PARTS, n_tok, width), f32),
            pltpu.VMEM((PARTS, 2 * team, width), bf16),
            pltpu.VMEM((PARTS, r, width), f32),
            pltpu.VMEM((PARTS, n_z * r, width), bf16),
            pltpu.VMEM((PARTS, n_z, r, width), bf16),
            pltpu.VMEM((PARTS, n_g, r, width), bf16),
        ]
        + [dma((3,)), dma((PARTS, 2)), dma((PARTS, 2)), dma((PARTS, n_z)), dma((PARTS, n_z))]
        + [dma((2 * n_s,))] * 2
        + [dma((PARTS,))] * 2
        + [dma((PARTS, n_s))] * 6
        + [dma((PARTS, n_z))] * 2
        + [dma((PARTS, n_g))] * 2
        + [dma((PARTS, n_s, 2))] * 2,
        compiler_params=pltpu.CompilerParams(
            collective_id=0, has_side_effects=True, vmem_limit_bytes=60 * 1024 * 1024
        ),
        cost_estimate=pl.CostEstimate(
            flops=4 * n_tok * depth_all * cols,
            bytes_accessed=4 * depth * cols,
            transcendentals=n_tok * cols // 2,
        ),
    )(tokens, panel, cotangent)
    return hidden, grad.astype(jnp.float32)


def solution(mesh):
    placed = (P(("dp", "tensor"), None), P("tensor", None), P(("dp", "tensor"), None))
    return jax.shard_map(
        on_device,
        mesh=mesh,
        in_specs=placed,
        out_specs=(P(("dp", "tensor"), None), P("tensor", None)),
        check_vma=False,
    )
```

```python
import functools
import math

import jax
import jax.numpy as jnp
from jax import lax
from jax.experimental import pallas as pl
from jax.experimental.pallas import tpu as pltpu
from jax.sharding import PartitionSpec as P

MESH = pl.DeviceIdType.MESH
PARTS = 2
LANES = 128


def repeat(low, high, body):
    if high - low <= 1:
        for i in range(low, high):
            body(i)
    else:
        lax.fori_loop(low, high, lambda i, carry: (body(i), carry)[1], 0)


def team_size(n_dp, depth):
    return max(s for s in range(1, n_dp + 1) if n_dp % s == 0 and depth % (s * LANES) == 0)


def kernel(
    n_dp, n_tensor, n_s, scale,
    tokens, panel, cotangent,
    hidden, grad,
    tok_v, ct_v, hid_v, stage, tok_x, tok_t, pan, mate_out, mate_in, sum_out, sum_in, own_part,
    proj, pre_all, row_own, row_out, row_in, team_in,
    in_sem, pan_sem, own_s, pan_s, pan_r, tok_s, tok_r, mate_s, mate_r, sum_s, sum_r,
    pre_s, pre_r, pair_s, pair_r, row_s, row_r, team_s, team_r, ag_s, ag_r,
):
    n_tok, _ = tokens.shape
    depth, cols = panel.shape
    width = cols // PARTS
    n_z = n_tensor // 2
    n_g = n_dp // n_s
    r = depth // n_s
    d, t = lax.axis_index("dp"), lax.axis_index("tensor")
    g, s = d // n_s, d % n_s
    z, c = t // 2, t % 2
    pair = z * 2 + 1 - c

    def send(src, dst, s_sem, r_sem, dp, tensor):
        return pltpu.make_async_remote_copy(
            src_ref=src, dst_ref=dst, send_sem=s_sem, recv_sem=r_sem,
            device_id=(dp, tensor), device_id_type=MESH,
        )

    def arrival(n):
        short = jnp.minimum(z, n_z - 1 - z)
        both = n < 2 * short
        m = jnp.where(both, n // 2 + 1, n - short + 1)
        side = jnp.where(both, 2 * (n % 2) - 1, jnp.where(z > n_z - 1 - z, -1, 1))
        return z + side * m, z - side

    def inside(place):
        return (place >= 0) & (place < n_z)

    def slots(i, size):
        return pl.ds(pl.multiple_of(i * size, size), size)

    def mate(j):
        return (s + j) % n_s

    def dp_of(i):
        return g * n_s + i

    units = cols // 2
    half = width // 2

    def columns(p, up):
        return pl.ds(up * units + p * half, half)

    def pan_in(p, up):
        return pltpu.make_async_copy(
            panel.at[slots(s, r), columns(p, up)],
            pan.at[p, slots(z, r), pl.ds(up * half, half)],
            pan_sem.at[p, up],
        )

    def pan_own(p, way):
        ref = pan.at[p, slots(z, r)]
        to = (z + 2 * way - 1) * 2 + c
        return send(ref, ref, own_s.at[p, way], pan_r.at[p, z], d, to)

    def pan_on(p, src, to):
        ref = pan.at[p, slots(src, r)]
        return send(ref, ref, pan_s.at[p, src], pan_r.at[p, src], d, to * 2 + c)

    my_slot = c * n_s + s

    def tok(k):
        e = (my_slot + k) % (2 * n_s)
        return send(
            stage.at[e], tok_x.at[slots(my_slot, n_tok)], tok_s.at[k], tok_r.at[k],
            dp_of(e % n_s), z * 2 + e // n_s,
        )

    def halfway(p):
        return send(mate_out.at[p], mate_in.at[p], mate_s.at[p], mate_r.at[p], d, pair)

    def sums(p, j):
        to = mate(j)
        return send(
            sum_out.at[p, slots(to, n_tok)], sum_in.at[p, j], sum_s.at[p, j], sum_r.at[p, j], dp_of(to), t
        )

    def pre(p, j, owner):
        ref = pre_all.at[p, slots(c * n_s + owner, n_tok)]
        return send(ref, ref, pre_s.at[p, j], pre_r.at[p, j], dp_of(mate(j)), t)

    def pre_pair(p, j, core):
        ref = pre_all.at[p, slots(core * n_s + mate(-j + n_s), n_tok)]
        return send(ref, ref, pair_s.at[p, j], pair_r.at[p, j], d, pair)

    def rows_to(p, k):
        to = (z + k) % n_z
        return send(
            row_out.at[p, slots(to, r)], row_in.at[p, k], row_s.at[p, k], row_r.at[p, k], d, to * 2 + c
        )

    def team(p, k):
        return send(
            team_in.at[p, g], team_in.at[p, g], team_s.at[p, k], team_r.at[p, k],
            ((g + k) % n_g) * n_s + s, t,
        )

    def ag(p, j, owner, up):
        ref = grad.at[slots(owner, r), columns(p, up)]
        return send(ref, ref, ag_s.at[p, j, up], ag_r.at[p, j, up], dp_of(mate(j)), t)

    def both_ways(copy, act):
        pl.when(z > 0)(lambda: act(copy(0)))
        pl.when(z < n_z - 1)(lambda: act(copy(1)))

    for p in range(PARTS):
        pan_in(p, 0).start()
        pan_in(p, 1).start()
    tokens_in = pltpu.make_async_copy(tokens, tok_v, in_sem.at[0])
    ct_in = pltpu.make_async_copy(cotangent, ct_v, in_sem.at[1])
    tokens_in.start()
    ct_in.start()

    barrier = pltpu.get_barrier_semaphore()

    def greet(dp, tensor):
        pl.semaphore_signal(barrier, inc=1, device_id=(dp, tensor), device_id_type=MESH)

    def greet_plane(k):
        e = (my_slot + k) % (2 * n_s)
        greet(dp_of(e % n_s), z * 2 + e // n_s)

    repeat(1, n_z, lambda k: greet(d, ((z + k) % n_z) * 2 + c))
    repeat(1, 2 * n_s, greet_plane)
    repeat(1, n_g, lambda k: greet(((g + k) % n_g) * n_s + s, t))
    pl.semaphore_wait(barrier, n_z + 2 * n_s + n_g - 3)

    def offer(p):
        pan_in(p, 0).wait()
        pan_in(p, 1).wait()
        both_ways(lambda way: pan_own(p, way), lambda copy: copy.start())

    offer(0)
    tokens_in.wait()

    for e in range(2 * n_s):
        for i in range(n_z):
            first = (i * 2 + e // n_s) * depth + (e % n_s) * r
            stage[e, :, i * r:(i + 1) * r] = tok_v[:, first:first + r]
    repeat(1, 2 * n_s, lambda k: tok(k).start())
    tok_x[slots(my_slot, n_tok), :] = stage[my_slot]
    ct_in.wait()

    def pass_on(p, n):
        src, to = arrival(n)
        pan_on(p, src, to).wait_recv()
        pl.when(inside(to))(lambda: pan_on(p, src, to).start())

    def take(k):
        ref = tok_x.at[slots((my_slot - k + 2 * n_s) % (2 * n_s), n_tok)]
        send(ref, ref, tok_s.at[k], tok_r.at[k], d, pair).wait_recv()

    def transpose(e):
        tok_t[:, slots(e, n_tok)] = tok_x[slots(e, n_tok), :].T

    tile = n_tok * max(i for i in (1, 2) if n_s % i == 0)
    tiles = n_s * n_tok // tile

    def partial(p):
        def one(i):
            core = lax.rem(i // tiles + 1 + c, 2)
            rows = slots(i % tiles, tile)
            own_part[rows, :] = jnp.dot(
                tok_x[slots(core * tiles + i % tiles, tile), :], pan[p],
                preferred_element_type=jnp.float32,
            )

            @pl.when(i < tiles)
            def _():
                mate_out[p, rows, :] = own_part[rows, :].astype(jnp.bfloat16)

            @pl.when(i == tiles - 1)
            def _():
                halfway(p).start()

        repeat(0, 2 * tiles, one)
        halfway(p).wait_recv()

        def add(j):
            rows = slots(mate(j), n_tok)
            own_part[rows, :] += mate_in[p, rows, :].astype(jnp.float32)
            sum_out[p, rows, :] = own_part[rows, :].astype(jnp.bfloat16)
            pl.when(j < n_s)(lambda: sums(p, j).start())

        repeat(1, n_s + 1, add)
        proj[p] = own_part[slots(s, n_tok), :]

    def activate(p):
        def add(j):
            sums(p, j).wait_recv()
            proj[p] += sum_in[p, j].astype(jnp.float32)

        repeat(1, n_s, add)
        gate = proj[p, :, :half]
        up = proj[p, :, half:]
        sig = jax.nn.sigmoid(gate)
        act = gate * sig
        ct = ct_v[:, p * half:(p + 1) * half].astype(jnp.float32)
        gate_grad = ct * up * sig * (1.0 + gate * (1.0 - sig))
        pre_all[p, slots(my_slot, n_tok), :half] = gate_grad.astype(jnp.bfloat16)
        pre_all[p, slots(my_slot, n_tok), half:] = (ct * act).astype(jnp.bfloat16)
        repeat(1, n_s, lambda j: pre(p, j, s).start())
        pre_pair(p, 0, c).start()
        hid_v[:, p * half:(p + 1) * half] = act * up

    def gather(p):
        def arrive(j):
            pre(p, j, mate(-j + n_s)).wait_recv()
            pre_pair(p, j, c).start()

        repeat(1, n_s, arrive)

    def product(p, k):
        to = (z + k) % n_z
        return scale * jnp.dot(
            tok_t[slots(to, r), :], pre_all[p], preferred_element_type=jnp.float32
        )

    def rows_out(p):
        repeat(0, n_s, lambda j: pre_pair(p, j, 1 - c).wait_recv())

        def product_out(k):
            row_out[p, slots((z + k) % n_z, r), :] = product(p, k).astype(jnp.bfloat16)
            pl.when(k < n_z)(lambda: rows_to(p, k).start())

        repeat(1, n_z + 1, product_out)

    def finish(p):
        own_rows = row_own.at[p]
        own_rows[...] = row_out[p, slots(z, r), :].astype(jnp.float32)

        def add(k):
            rows_to(p, k).wait_recv()
            own_rows[...] += row_in[p, k].astype(jnp.float32)

        repeat(1, n_z, add)
        if n_g > 1:
            team_in[p, g] = own_rows[...].astype(jnp.bfloat16)
            repeat(1, n_g, lambda k: team(p, k).start())

            def others(k):
                ref = team_in.at[p, (g - k + n_g) % n_g]
                send(ref, ref, team_s.at[p, k], team_r.at[p, k], d, pair).wait_recv()

            repeat(1, n_g, others)
            own_rows[...] = jnp.zeros((r, width), jnp.float32)

            def add_team(i):
                own_rows[...] += team_in[p, i].astype(jnp.float32)

            repeat(0, n_g, add_team)
        for up in range(2):
            grad[slots(s, r), columns(p, up)] = own_rows[:, up * half:(up + 1) * half].astype(jnp.bfloat16)
            repeat(1, n_s, lambda j: ag(p, j, s, up).start())

    hidden_out = pltpu.make_async_copy(hid_v, hidden, in_sem.at[2])

    z_time, xy_time, sum_time = 16.0 / PARTS, 10.5 / PARTS, 21.0 / PARTS
    plan = []
    for p in range(PARTS):
        for n in range(n_z - 1):
            plan.append((z_time * (p + (n + 1) / (n_z - 1)) + 1.0 + n / n_z, functools.partial(pass_on, p, n)))
            if n == 0 and p + 1 < PARTS:
                plan.append((plan[-1][0] + 0.01, functools.partial(offer, p + 1)))
        ready = z_time * (p + 1) + 2.0
        plan.append((ready, functools.partial(partial, p)))
        ready = max(ready + 3.0, 13.0 + xy_time * p) + xy_time
        plan.append((ready, functools.partial(activate, p)))
        ready = ready + 1.5 + xy_time
        plan.append((ready, functools.partial(gather, p)))
        ready = ready + 1.0
        plan.append((ready, functools.partial(rows_out, p)))
        ready = max(ready + 1.5, 27.0 + sum_time * p) + sum_time
        plan.append((ready, functools.partial(finish, p)))
    last_partial = z_time * PARTS + 2.0
    plan.append((z_time + 1.99, lambda: repeat(1, 2 * n_s, take)))
    plan.append((last_partial + 0.01, lambda: repeat(0, 2 * n_s, transpose)))
    for _, run in sorted(plan, key=lambda item: item[0]):
        run()
    hidden_out.start()
    for p in range(PARTS):
        for up in range(2):
            repeat(1, n_s, lambda j: ag(p, j, mate(-j + n_s), up).wait_recv())

    hidden_out.wait()
    repeat(1, 2 * n_s, lambda k: tok(k).wait_send())
    for p in range(PARTS):
        both_ways(lambda way: pan_own(p, way), lambda copy: copy.wait_send())

        def passed_on(n):
            src, to = arrival(n)
            pl.when(inside(to))(lambda: pan_on(p, src, to).wait_send())

        repeat(0, n_z - 1, passed_on)
        halfway(p).wait_send()
        repeat(1, n_z, lambda k: rows_to(p, k).wait_send())
        repeat(1, n_g, lambda k: team(p, k).wait_send())
        repeat(0, n_s, lambda j: pre_pair(p, j, c).wait_send())

        def sent(j):
            sums(p, j).wait_send()
            pre(p, j, s).wait_send()
            ag(p, j, s, 0).wait_send()
            ag(p, j, s, 1).wait_send()

        repeat(1, n_s, sent)


def on_device(tokens, panel, cotangent):
    n_tok, depth_all = tokens.shape
    depth, cols = panel.shape
    n_tensor = lax.axis_size("tensor")
    n_dp = lax.axis_size("dp")
    n_z = n_tensor // 2
    n_s = team_size(n_dp, depth)
    n_g = n_dp // n_s
    r = depth // n_s
    scale = 1.0 / math.sqrt(n_tok * n_tensor * n_dp)
    width = cols // PARTS
    team = n_s * n_tok
    dma = pltpu.SemaphoreType.DMA
    anywhere = pl.BlockSpec(memory_space=pl.ANY)
    bf16, f32 = jnp.bfloat16, jnp.float32
    hidden, grad = pl.pallas_call(
        functools.partial(kernel, n_dp, n_tensor, n_s, scale),
        out_shape=(
            jax.ShapeDtypeStruct((n_tok, cols // 2), f32),
            jax.ShapeDtypeStruct((depth, cols), bf16),
        ),
        in_specs=[anywhere] * 3,
        out_specs=(anywhere, pl.BlockSpec(memory_space=pltpu.VMEM)),
        scratch_shapes=[
            pltpu.VMEM((n_tok, depth_all), bf16),
            pltpu.VMEM((n_tok, cols // 2), bf16),
            pltpu.VMEM((n_tok, cols // 2), f32),
            pltpu.VMEM((2 * n_s, n_tok, n_z * r), bf16),
            pltpu.VMEM((2 * team, n_z * r), bf16),
            pltpu.VMEM((n_z * r, 2 * team), bf16),
            pltpu.VMEM((PARTS, n_z * r, width), bf16),
            pltpu.VMEM((PARTS, team, width), bf16),
            pltpu.VMEM((PARTS, team, width), bf16),
            pltpu.VMEM((PARTS, team, width), bf16),
            pltpu.VMEM((PARTS, n_s, n_tok, width), bf16),
            pltpu.VMEM((team, width), f32),
            pltpu.VMEM((PARTS, n_tok, width), f32),
            pltpu.VMEM((PARTS, 2 * team, width), bf16),
            pltpu.VMEM((PARTS, r, width), f32),
            pltpu.VMEM((PARTS, n_z * r, width), bf16),
            pltpu.VMEM((PARTS, n_z, r, width), bf16),
            pltpu.VMEM((PARTS, n_g, r, width), bf16),
        ]
        + [dma((3,)), dma((PARTS, 2)), dma((PARTS, 2)), dma((PARTS, n_z)), dma((PARTS, n_z))]
        + [dma((2 * n_s,))] * 2
        + [dma((PARTS,))] * 2
        + [dma((PARTS, n_s))] * 6
        + [dma((PARTS, n_z))] * 2
        + [dma((PARTS, n_g))] * 2
        + [dma((PARTS, n_s, 2))] * 2,
        compiler_params=pltpu.CompilerParams(
            collective_id=0, has_side_effects=True, vmem_limit_bytes=60 * 1024 * 1024
        ),
        cost_estimate=pl.CostEstimate(
            flops=4 * n_tok * depth_all * cols,
            bytes_accessed=4 * depth * cols,
            transcendentals=n_tok * cols // 2,
        ),
    )(tokens, panel, cotangent)
    return hidden, grad.astype(jnp.float32)


def solution(mesh):
    placed = (P(("dp", "tensor"), None), P("tensor", None), P(("dp", "tensor"), None))
    return jax.shard_map(
        on_device,
        mesh=mesh,
        in_specs=placed,
        out_specs=(P(("dp", "tensor"), None), P("tensor", None)),
        check_vma=False,
    )
```

```python
import functools
import math

import jax
import jax.numpy as jnp
from jax import lax
from jax.experimental import pallas as pl
from jax.experimental.pallas import tpu as pltpu
from jax.sharding import PartitionSpec as P

MESH = pl.DeviceIdType.MESH
PARTS = 2
LANES = 128


def repeat(low, high, body):
    if high - low <= 1:
        for i in range(low, high):
            body(i)
    else:
        lax.fori_loop(low, high, lambda i, carry: (body(i), carry)[1], 0)


def team_size(n_dp, depth):
    return max(s for s in range(1, n_dp + 1) if n_dp % s == 0 and depth % (s * LANES) == 0)


def kernel(
    n_dp, n_tensor, n_s, scale,
    tokens, panel, cotangent,
    hidden, grad,
    tok_v, ct_v, hid_v, stage, tok_x, tok_t, pan, mate_out, mate_in, sum_out, sum_in, own_part,
    proj, pre_all, row_own, row_out, row_in, team_in,
    in_sem, pan_sem, pan_s, pan_r, tok_s, tok_r, mate_s, mate_r, sum_s, sum_r,
    pre_s, pre_r, pair_s, pair_r, row_s, row_r, team_s, team_r, ag_s, ag_r,
):
    n_tok, _ = tokens.shape
    depth, cols = panel.shape
    width = cols // PARTS
    n_z = n_tensor // 2
    n_g = n_dp // n_s
    r = depth // n_s
    d, t = lax.axis_index("dp"), lax.axis_index("tensor")
    g, s = d // n_s, d % n_s
    z, c = t // 2, t % 2
    pair = z * 2 + 1 - c

    def send(src, dst, s_sem, r_sem, dp, tensor):
        return pltpu.make_async_remote_copy(
            src_ref=src, dst_ref=dst, send_sem=s_sem, recv_sem=r_sem,
            device_id=(dp, tensor), device_id_type=MESH,
        )

    def slots(i, size):
        return pl.ds(pl.multiple_of(i * size, size), size)

    def mate(j):
        return (s + j) % n_s

    def dp_of(i):
        return g * n_s + i

    units = cols // 2
    half = width // 2

    def columns(p, up):
        return pl.ds(up * units + p * half, half)

    def pan_in(p, up):
        return pltpu.make_async_copy(
            panel.at[slots(s, r), columns(p, up)],
            pan.at[p, slots(z, r), pl.ds(up * half, half)],
            pan_sem.at[p, up],
        )

    def pan_to(p, k):
        ref = pan.at[p, slots(z, r)]
        return send(ref, ref, pan_s.at[p, k], pan_r.at[p, k], d, ((z + k) % n_z) * 2 + c)

    def pan_from(p, k):
        ref = pan.at[p, slots((z - k + n_z) % n_z, r)]
        return send(ref, ref, pan_s.at[p, k], pan_r.at[p, k], d, pair)

    my_slot = c * n_s + s

    def tok(k):
        e = (my_slot + k) % (2 * n_s)
        return send(
            stage.at[e], tok_x.at[slots(my_slot, n_tok)], tok_s.at[k], tok_r.at[k],
            dp_of(e % n_s), z * 2 + e // n_s,
        )

    def halfway(p):
        return send(mate_out.at[p], mate_in.at[p], mate_s.at[p], mate_r.at[p], d, pair)

    def sums(p, j):
        to = mate(j)
        return send(
            sum_out.at[p, slots(to, n_tok)], sum_in.at[p, j], sum_s.at[p, j], sum_r.at[p, j], dp_of(to), t
        )

    def pre(p, j, owner):
        ref = pre_all.at[p, slots(c * n_s + owner, n_tok)]
        return send(ref, ref, pre_s.at[p, j], pre_r.at[p, j], dp_of(mate(j)), t)

    def pre_pair(p, j, core):
        ref = pre_all.at[p, slots(core * n_s + mate(-j + n_s), n_tok)]
        return send(ref, ref, pair_s.at[p, j], pair_r.at[p, j], d, pair)

    def rows_to(p, k):
        to = (z + k) % n_z
        return send(
            row_out.at[p, slots(to, r)], row_in.at[p, k], row_s.at[p, k], row_r.at[p, k], d, to * 2 + c
        )

    def team(p, k):
        return send(
            team_in.at[p, g], team_in.at[p, g], team_s.at[p, k], team_r.at[p, k],
            ((g + k) % n_g) * n_s + s, t,
        )

    def ag(p, j, owner, up):
        ref = grad.at[slots(owner, r), columns(p, up)]
        return send(ref, ref, ag_s.at[p, j, up], ag_r.at[p, j, up], dp_of(mate(j)), t)

    for p in range(PARTS):
        pan_in(p, 0).start()
        pan_in(p, 1).start()
    tokens_in = pltpu.make_async_copy(tokens, tok_v, in_sem.at[0])
    ct_in = pltpu.make_async_copy(cotangent, ct_v, in_sem.at[1])
    tokens_in.start()
    ct_in.start()

    barrier = pltpu.get_barrier_semaphore()

    def greet(dp, tensor):
        pl.semaphore_signal(barrier, inc=1, device_id=(dp, tensor), device_id_type=MESH)

    def greet_plane(k):
        e = (my_slot + k) % (2 * n_s)
        greet(dp_of(e % n_s), z * 2 + e // n_s)

    repeat(1, n_z, lambda k: greet(d, ((z + k) % n_z) * 2 + c))
    repeat(1, 2 * n_s, greet_plane)
    repeat(1, n_g, lambda k: greet(((g + k) % n_g) * n_s + s, t))
    pl.semaphore_wait(barrier, n_z + 2 * n_s + n_g - 3)

    def offer(p):
        pan_in(p, 0).wait()
        pan_in(p, 1).wait()
        repeat(1, n_z, lambda k: pan_to(p, k).start())

    offer(0)
    tokens_in.wait()

    for e in range(2 * n_s):
        for i in range(n_z):
            first = (i * 2 + e // n_s) * depth + (e % n_s) * r
            stage[e, :, i * r:(i + 1) * r] = tok_v[:, first:first + r]
    repeat(1, 2 * n_s, lambda k: tok(k).start())
    tok_x[slots(my_slot, n_tok), :] = stage[my_slot]
    ct_in.wait()

    def collect(p, low, high):
        repeat(low, high, lambda k: pan_from(p, k).wait_recv())

    def take(k):
        ref = tok_x.at[slots((my_slot - k + 2 * n_s) % (2 * n_s), n_tok)]
        send(ref, ref, tok_s.at[k], tok_r.at[k], d, pair).wait_recv()

    def transpose(e):
        tok_t[:, slots(e, n_tok)] = tok_x[slots(e, n_tok), :].T

    tile = n_tok * max(i for i in (1, 2) if n_s % i == 0)
    tiles = n_s * n_tok // tile

    def partial(p):
        def one(i):
            core = lax.rem(i // tiles + 1 + c, 2)
            rows = slots(i % tiles, tile)
            own_part[rows, :] = jnp.dot(
                tok_x[slots(core * tiles + i % tiles, tile), :], pan[p],
                preferred_element_type=jnp.float32,
            )

            @pl.when(i < tiles)
            def _():
                mate_out[p, rows, :] = own_part[rows, :].astype(jnp.bfloat16)

            @pl.when(i == tiles - 1)
            def _():
                halfway(p).start()

        repeat(0, 2 * tiles, one)
        halfway(p).wait_recv()

        def add(j):
            rows = slots(mate(j), n_tok)
            own_part[rows, :] += mate_in[p, rows, :].astype(jnp.float32)
            sum_out[p, rows, :] = own_part[rows, :].astype(jnp.bfloat16)
            pl.when(j < n_s)(lambda: sums(p, j).start())

        repeat(1, n_s + 1, add)
        proj[p] = own_part[slots(s, n_tok), :]

    def activate(p):
        def add(j):
            sums(p, j).wait_recv()
            proj[p] += sum_in[p, j].astype(jnp.float32)

        repeat(1, n_s, add)
        gate = proj[p, :, :half]
        up = proj[p, :, half:]
        sig = jax.nn.sigmoid(gate)
        act = gate * sig
        ct = ct_v[:, p * half:(p + 1) * half].astype(jnp.float32)
        gate_grad = ct * up * sig * (1.0 + gate * (1.0 - sig))
        pre_all[p, slots(my_slot, n_tok), :half] = gate_grad.astype(jnp.bfloat16)
        pre_all[p, slots(my_slot, n_tok), half:] = (ct * act).astype(jnp.bfloat16)
        repeat(1, n_s, lambda j: pre(p, j, s).start())
        pre_pair(p, 0, c).start()
        hid_v[:, p * half:(p + 1) * half] = act * up

    def gather(p):
        def arrive(j):
            pre(p, j, mate(-j + n_s)).wait_recv()
            pre_pair(p, j, c).start()

        repeat(1, n_s, arrive)

    def product(p, k):
        to = (z + k) % n_z
        return scale * jnp.dot(
            tok_t[slots(to, r), :], pre_all[p], preferred_element_type=jnp.float32
        )

    def rows_out(p):
        repeat(0, n_s, lambda j: pre_pair(p, j, 1 - c).wait_recv())

        def product_out(k):
            row_out[p, slots((z + k) % n_z, r), :] = product(p, k).astype(jnp.bfloat16)
            pl.when(k < n_z)(lambda: rows_to(p, k).start())

        repeat(1, n_z + 1, product_out)

    def finish(p):
        own_rows = row_own.at[p]
        own_rows[...] = row_out[p, slots(z, r), :].astype(jnp.float32)

        def add(k):
            rows_to(p, k).wait_recv()
            own_rows[...] += row_in[p, k].astype(jnp.float32)

        repeat(1, n_z, add)
        if n_g > 1:
            team_in[p, g] = own_rows[...].astype(jnp.bfloat16)
            repeat(1, n_g, lambda k: team(p, k).start())

            def others(k):
                ref = team_in.at[p, (g - k + n_g) % n_g]
                send(ref, ref, team_s.at[p, k], team_r.at[p, k], d, pair).wait_recv()

            repeat(1, n_g, others)
            own_rows[...] = jnp.zeros((r, width), jnp.float32)

            def add_team(i):
                own_rows[...] += team_in[p, i].astype(jnp.float32)

            repeat(0, n_g, add_team)
        for up in range(2):
            grad[slots(s, r), columns(p, up)] = own_rows[:, up * half:(up + 1) * half].astype(jnp.bfloat16)
            repeat(1, n_s, lambda j: ag(p, j, s, up).start())

    hidden_out = pltpu.make_async_copy(hid_v, hidden, in_sem.at[2])

    z_time, xy_time, sum_time = 21.0 / PARTS, 10.5 / PARTS, 21.0 / PARTS
    plan = []
    for p in range(PARTS):
        plan.append((z_time * (p + 0.4), functools.partial(collect, p, 1, 2)))
        if p + 1 < PARTS:
            plan.append((z_time * (p + 0.41), functools.partial(offer, p + 1)))
        plan.append((z_time * (p + 1) + 1.0, functools.partial(collect, p, 2, n_z)))
        ready = z_time * (p + 1) + 2.0
        plan.append((ready, functools.partial(partial, p)))
        ready = max(ready + 3.0, 13.0 + xy_time * p) + xy_time
        plan.append((ready, functools.partial(activate, p)))
        ready = ready + 1.5 + xy_time
        plan.append((ready, functools.partial(gather, p)))
        ready = ready + 1.0
        plan.append((ready, functools.partial(rows_out, p)))
        ready = max(ready + 1.5, 30.0 + sum_time * p) + sum_time
        plan.append((ready, functools.partial(finish, p)))
    last_partial = z_time * PARTS + 2.0
    plan.append((z_time + 1.99, lambda: repeat(1, 2 * n_s, take)))
    plan.append((last_partial + 0.01, lambda: repeat(0, 2 * n_s, transpose)))
    for _, run in sorted(plan, key=lambda item: item[0]):
        run()
    hidden_out.start()
    for p in range(PARTS):
        for up in range(2):
            repeat(1, n_s, lambda j: ag(p, j, mate(-j + n_s), up).wait_recv())

    hidden_out.wait()
    repeat(1, 2 * n_s, lambda k: tok(k).wait_send())
    for p in range(PARTS):
        repeat(1, n_z, lambda k: pan_to(p, k).wait_send())
        halfway(p).wait_send()
        repeat(1, n_z, lambda k: rows_to(p, k).wait_send())
        repeat(1, n_g, lambda k: team(p, k).wait_send())
        repeat(0, n_s, lambda j: pre_pair(p, j, c).wait_send())

        def sent(j):
            sums(p, j).wait_send()
            pre(p, j, s).wait_send()
            ag(p, j, s, 0).wait_send()
            ag(p, j, s, 1).wait_send()

        repeat(1, n_s, sent)


def on_device(tokens, panel, cotangent):
    n_tok, depth_all = tokens.shape
    depth, cols = panel.shape
    n_tensor = lax.axis_size("tensor")
    n_dp = lax.axis_size("dp")
    n_z = n_tensor // 2
    n_s = team_size(n_dp, depth)
    n_g = n_dp // n_s
    r = depth // n_s
    scale = 1.0 / math.sqrt(n_tok * n_tensor * n_dp)
    width = cols // PARTS
    team = n_s * n_tok
    dma = pltpu.SemaphoreType.DMA
    anywhere = pl.BlockSpec(memory_space=pl.ANY)
    bf16, f32 = jnp.bfloat16, jnp.float32
    hidden, grad = pl.pallas_call(
        functools.partial(kernel, n_dp, n_tensor, n_s, scale),
        out_shape=(
            jax.ShapeDtypeStruct((n_tok, cols // 2), f32),
            jax.ShapeDtypeStruct((depth, cols), bf16),
        ),
        in_specs=[anywhere] * 3,
        out_specs=(anywhere, pl.BlockSpec(memory_space=pltpu.VMEM)),
        scratch_shapes=[
            pltpu.VMEM((n_tok, depth_all), bf16),
            pltpu.VMEM((n_tok, cols // 2), bf16),
            pltpu.VMEM((n_tok, cols // 2), f32),
            pltpu.VMEM((2 * n_s, n_tok, n_z * r), bf16),
            pltpu.VMEM((2 * team, n_z * r), bf16),
            pltpu.VMEM((n_z * r, 2 * team), bf16),
            pltpu.VMEM((PARTS, n_z * r, width), bf16),
            pltpu.VMEM((PARTS, team, width), bf16),
            pltpu.VMEM((PARTS, team, width), bf16),
            pltpu.VMEM((PARTS, team, width), bf16),
            pltpu.VMEM((PARTS, n_s, n_tok, width), bf16),
            pltpu.VMEM((team, width), f32),
            pltpu.VMEM((PARTS, n_tok, width), f32),
            pltpu.VMEM((PARTS, 2 * team, width), bf16),
            pltpu.VMEM((PARTS, r, width), f32),
            pltpu.VMEM((PARTS, n_z * r, width), bf16),
            pltpu.VMEM((PARTS, n_z, r, width), bf16),
            pltpu.VMEM((PARTS, n_g, r, width), bf16),
        ]
        + [dma((3,)), dma((PARTS, 2)), dma((PARTS, n_z)), dma((PARTS, n_z))]
        + [dma((2 * n_s,))] * 2
        + [dma((PARTS,))] * 2
        + [dma((PARTS, n_s))] * 6
        + [dma((PARTS, n_z))] * 2
        + [dma((PARTS, n_g))] * 2
        + [dma((PARTS, n_s, 2))] * 2,
        compiler_params=pltpu.CompilerParams(
            collective_id=0, has_side_effects=True, vmem_limit_bytes=60 * 1024 * 1024
        ),
        cost_estimate=pl.CostEstimate(
            flops=4 * n_tok * depth_all * cols,
            bytes_accessed=4 * depth * cols,
            transcendentals=n_tok * cols // 2,
        ),
    )(tokens, panel, cotangent)
    return hidden, grad.astype(jnp.float32)


def solution(mesh):
    placed = (P(("dp", "tensor"), None), P("tensor", None), P(("dp", "tensor"), None))
    return jax.shard_map(
        on_device,
        mesh=mesh,
        in_specs=placed,
        out_specs=(P(("dp", "tensor"), None), P("tensor", None)),
        check_vma=False,
    )
```

```python
import functools
import math

import jax
import jax.numpy as jnp
from jax import lax
from jax.experimental import pallas as pl
from jax.experimental.pallas import tpu as pltpu
from jax.sharding import PartitionSpec as P

MESH = pl.DeviceIdType.MESH
PARTS = 4
LANES = 128


def repeat(low, high, body):
    if high - low <= 1:
        for i in range(low, high):
            body(i)
    else:
        lax.fori_loop(low, high, lambda i, carry: (body(i), carry)[1], 0)


def team_size(n_dp, depth):
    return max(s for s in range(1, n_dp + 1) if n_dp % s == 0 and depth % (s * LANES) == 0)


def kernel(
    n_dp, n_tensor, n_s, scale,
    tokens, panel, cotangent,
    hidden, grad,
    tok_v, ct_v, hid_v, stage, tok_x, tok_t, pan, mate_out, mate_in, sum_out, sum_in, own_part,
    proj, pre_all, row_own, row_out, row_in, team_in,
    in_sem, pan_sem, pan_s, pan_r, tok_s, tok_r, mate_s, mate_r, sum_s, sum_r,
    pre_s, pre_r, pair_s, pair_r, row_s, row_r, team_s, team_r, ag_s, ag_r,
):
    n_tok, _ = tokens.shape
    depth, cols = panel.shape
    width = cols // PARTS
    n_z = n_tensor // 2
    n_g = n_dp // n_s
    r = depth // n_s
    d, t = lax.axis_index("dp"), lax.axis_index("tensor")
    g, s = d // n_s, d % n_s
    z, c = t // 2, t % 2
    pair = z * 2 + 1 - c

    def send(src, dst, s_sem, r_sem, dp, tensor):
        return pltpu.make_async_remote_copy(
            src_ref=src, dst_ref=dst, send_sem=s_sem, recv_sem=r_sem,
            device_id=(dp, tensor), device_id_type=MESH,
        )

    def slots(i, size):
        return pl.ds(pl.multiple_of(i * size, size), size)

    def mate(j):
        return (s + j) % n_s

    def dp_of(i):
        return g * n_s + i

    units = cols // 2
    half = width // 2

    def columns(p, up):
        return pl.ds(up * units + p * half, half)

    def pan_in(p, up):
        return pltpu.make_async_copy(
            panel.at[slots(s, r), columns(p, up)],
            pan.at[p, slots(z, r), pl.ds(up * half, half)],
            pan_sem.at[p, up],
        )

    def pan_to(p, k):
        ref = pan.at[p, slots(z, r)]
        return send(ref, ref, pan_s.at[p, k], pan_r.at[p, k], d, ((z + k) % n_z) * 2 + c)

    def pan_from(p, k):
        ref = pan.at[p, slots((z - k + n_z) % n_z, r)]
        return send(ref, ref, pan_s.at[p, k], pan_r.at[p, k], d, pair)

    my_slot = c * n_s + s

    def tok(k):
        e = (my_slot + k) % (2 * n_s)
        return send(
            stage.at[e], tok_x.at[slots(my_slot, n_tok)], tok_s.at[k], tok_r.at[k],
            dp_of(e % n_s), z * 2 + e // n_s,
        )

    def halfway(p):
        return send(mate_out.at[p], mate_in.at[p], mate_s.at[p], mate_r.at[p], d, pair)

    def sums(p, j):
        to = mate(j)
        return send(
            sum_out.at[p, slots(to, n_tok)], sum_in.at[p, j], sum_s.at[p, j], sum_r.at[p, j], dp_of(to), t
        )

    def pre(p, j, owner):
        ref = pre_all.at[p, slots(c * n_s + owner, n_tok)]
        return send(ref, ref, pre_s.at[p, j], pre_r.at[p, j], dp_of(mate(j)), t)

    def pre_pair(p, j, core):
        ref = pre_all.at[p, slots(core * n_s + mate(-j + n_s), n_tok)]
        return send(ref, ref, pair_s.at[p, j], pair_r.at[p, j], d, pair)

    def rows_to(p, k):
        to = (z + k) % n_z
        return send(
            row_out.at[p, slots(to, r)], row_in.at[p, k], row_s.at[p, k], row_r.at[p, k], d, to * 2 + c
        )

    def team(p, k):
        return send(
            team_in.at[p, g], team_in.at[p, g], team_s.at[p, k], team_r.at[p, k],
            ((g + k) % n_g) * n_s + s, t,
        )

    def ag(p, j, owner, up):
        ref = grad.at[slots(owner, r), columns(p, up)]
        return send(ref, ref, ag_s.at[p, j, up], ag_r.at[p, j, up], dp_of(mate(j)), t)

    for p in range(PARTS):
        pan_in(p, 0).start()
        pan_in(p, 1).start()
    tokens_in = pltpu.make_async_copy(tokens, tok_v, in_sem.at[0])
    ct_in = pltpu.make_async_copy(cotangent, ct_v, in_sem.at[1])
    tokens_in.start()
    ct_in.start()

    barrier = pltpu.get_barrier_semaphore()

    def greet(dp, tensor):
        pl.semaphore_signal(barrier, inc=1, device_id=(dp, tensor), device_id_type=MESH)

    def greet_plane(k):
        e = (my_slot + k) % (2 * n_s)
        greet(dp_of(e % n_s), z * 2 + e // n_s)

    repeat(1, n_z, lambda k: greet(d, ((z + k) % n_z) * 2 + c))
    repeat(1, 2 * n_s, greet_plane)
    repeat(1, n_g, lambda k: greet(((g + k) % n_g) * n_s + s, t))
    pl.semaphore_wait(barrier, n_z + 2 * n_s + n_g - 3)

    def offer(p):
        pan_in(p, 0).wait()
        pan_in(p, 1).wait()
        repeat(1, n_z, lambda k: pan_to(p, k).start())

    offer(0)
    tokens_in.wait()

    for e in range(2 * n_s):
        for i in range(n_z):
            first = (i * 2 + e // n_s) * depth + (e % n_s) * r
            stage[e, :, i * r:(i + 1) * r] = tok_v[:, first:first + r]
    repeat(1, 2 * n_s, lambda k: tok(k).start())
    tok_x[slots(my_slot, n_tok), :] = stage[my_slot]
    ct_in.wait()

    def collect(p, low, high):
        repeat(low, high, lambda k: pan_from(p, k).wait_recv())

    def take(k):
        ref = tok_x.at[slots((my_slot - k + 2 * n_s) % (2 * n_s), n_tok)]
        send(ref, ref, tok_s.at[k], tok_r.at[k], d, pair).wait_recv()

    def transpose(e):
        tok_t[:, slots(e, n_tok)] = tok_x[slots(e, n_tok), :].T

    tile = n_tok * max(i for i in (1, 2) if n_s % i == 0)
    tiles = n_s * n_tok // tile

    def partial(p):
        def one(i):
            core = lax.rem(i // tiles + 1 + c, 2)
            rows = slots(i % tiles, tile)
            own_part[rows, :] = jnp.dot(
                tok_x[slots(core * tiles + i % tiles, tile), :], pan[p],
                preferred_element_type=jnp.float32,
            )

            @pl.when(i < tiles)
            def _():
                mate_out[p, rows, :] = own_part[rows, :].astype(jnp.bfloat16)

            @pl.when(i == tiles - 1)
            def _():
                halfway(p).start()

        repeat(0, 2 * tiles, one)
        halfway(p).wait_recv()

        def add(j):
            rows = slots(mate(j), n_tok)
            own_part[rows, :] += mate_in[p, rows, :].astype(jnp.float32)
            sum_out[p, rows, :] = own_part[rows, :].astype(jnp.bfloat16)
            pl.when(j < n_s)(lambda: sums(p, j).start())

        repeat(1, n_s + 1, add)
        proj[p] = own_part[slots(s, n_tok), :]

    def activate(p):
        def add(j):
            sums(p, j).wait_recv()
            proj[p] += sum_in[p, j].astype(jnp.float32)

        repeat(1, n_s, add)
        gate = proj[p, :, :half]
        up = proj[p, :, half:]
        sig = jax.nn.sigmoid(gate)
        act = gate * sig
        ct = ct_v[:, p * half:(p + 1) * half].astype(jnp.float32)
        gate_grad = ct * up * sig * (1.0 + gate * (1.0 - sig))
        pre_all[p, slots(my_slot, n_tok), :half] = gate_grad.astype(jnp.bfloat16)
        pre_all[p, slots(my_slot, n_tok), half:] = (ct * act).astype(jnp.bfloat16)
        repeat(1, n_s, lambda j: pre(p, j, s).start())
        pre_pair(p, 0, c).start()
        hid_v[:, p * half:(p + 1) * half] = act * up

    def gather(p):
        def arrive(j):
            pre(p, j, mate(-j + n_s)).wait_recv()
            pre_pair(p, j, c).start()

        repeat(1, n_s, arrive)

    def product(p, k):
        to = (z + k) % n_z
        return scale * jnp.dot(
            tok_t[slots(to, r), :], pre_all[p], preferred_element_type=jnp.float32
        )

    def rows_out(p):
        repeat(0, n_s, lambda j: pre_pair(p, j, 1 - c).wait_recv())

        def product_out(k):
            row_out[p, slots((z + k) % n_z, r), :] = product(p, k).astype(jnp.bfloat16)
            pl.when(k < n_z)(lambda: rows_to(p, k).start())

        repeat(1, n_z + 1, product_out)

    def finish(p):
        own_rows = row_own.at[p]
        own_rows[...] = row_out[p, slots(z, r), :].astype(jnp.float32)

        def add(k):
            rows_to(p, k).wait_recv()
            own_rows[...] += row_in[p, k].astype(jnp.float32)

        repeat(1, n_z, add)
        if n_g > 1:
            team_in[p, g] = own_rows[...].astype(jnp.bfloat16)
            repeat(1, n_g, lambda k: team(p, k).start())

            def others(k):
                ref = team_in.at[p, (g - k + n_g) % n_g]
                send(ref, ref, team_s.at[p, k], team_r.at[p, k], d, pair).wait_recv()

            repeat(1, n_g, others)
            own_rows[...] = jnp.zeros((r, width), jnp.float32)

            def add_team(i):
                own_rows[...] += team_in[p, i].astype(jnp.float32)

            repeat(0, n_g, add_team)
        for up in range(2):
            grad[slots(s, r), columns(p, up)] = own_rows[:, up * half:(up + 1) * half].astype(jnp.bfloat16)
            repeat(1, n_s, lambda j: ag(p, j, s, up).start())

    hidden_out = pltpu.make_async_copy(hid_v, hidden, in_sem.at[2])

    z_time, xy_time, sum_time = 21.0 / PARTS, 10.5 / PARTS, 21.0 / PARTS
    plan = []
    for p in range(PARTS):
        plan.append((z_time * (p + 0.4), functools.partial(collect, p, 1, 2)))
        if p + 1 < PARTS:
            plan.append((z_time * (p + 0.41), functools.partial(offer, p + 1)))
        plan.append((z_time * (p + 1) + 1.0, functools.partial(collect, p, 2, n_z)))
        ready = z_time * (p + 1) + 2.0
        plan.append((ready, functools.partial(partial, p)))
        ready = max(ready + 3.0, 13.0 + xy_time * p) + xy_time
        plan.append((ready, functools.partial(activate, p)))
        ready = ready + 1.5 + xy_time
        plan.append((ready, functools.partial(gather, p)))
        ready = ready + 1.0
        plan.append((ready, functools.partial(rows_out, p)))
        ready = max(ready + 1.5, 30.0 + sum_time * p) + sum_time
        plan.append((ready, functools.partial(finish, p)))
    plan.append((z_time + 1.99, lambda: repeat(1, 2 * n_s, take)))
    plan.append((z_time + 2.01, lambda: repeat(0, 2 * n_s, transpose)))
    for _, run in sorted(plan, key=lambda item: item[0]):
        run()
    hidden_out.start()
    for p in range(PARTS):
        for up in range(2):
            repeat(1, n_s, lambda j: ag(p, j, mate(-j + n_s), up).wait_recv())

    hidden_out.wait()
    repeat(1, 2 * n_s, lambda k: tok(k).wait_send())
    for p in range(PARTS):
        repeat(1, n_z, lambda k: pan_to(p, k).wait_send())
        halfway(p).wait_send()
        repeat(1, n_z, lambda k: rows_to(p, k).wait_send())
        repeat(1, n_g, lambda k: team(p, k).wait_send())
        repeat(0, n_s, lambda j: pre_pair(p, j, c).wait_send())

        def sent(j):
            sums(p, j).wait_send()
            pre(p, j, s).wait_send()
            ag(p, j, s, 0).wait_send()
            ag(p, j, s, 1).wait_send()

        repeat(1, n_s, sent)


def on_device(tokens, panel, cotangent):
    n_tok, depth_all = tokens.shape
    depth, cols = panel.shape
    n_tensor = lax.axis_size("tensor")
    n_dp = lax.axis_size("dp")
    n_z = n_tensor // 2
    n_s = team_size(n_dp, depth)
    n_g = n_dp // n_s
    r = depth // n_s
    scale = 1.0 / math.sqrt(n_tok * n_tensor * n_dp)
    width = cols // PARTS
    team = n_s * n_tok
    dma = pltpu.SemaphoreType.DMA
    anywhere = pl.BlockSpec(memory_space=pl.ANY)
    bf16, f32 = jnp.bfloat16, jnp.float32
    hidden, grad = pl.pallas_call(
        functools.partial(kernel, n_dp, n_tensor, n_s, scale),
        out_shape=(
            jax.ShapeDtypeStruct((n_tok, cols // 2), f32),
            jax.ShapeDtypeStruct((depth, cols), bf16),
        ),
        in_specs=[anywhere] * 3,
        out_specs=(anywhere, pl.BlockSpec(memory_space=pltpu.VMEM)),
        scratch_shapes=[
            pltpu.VMEM((n_tok, depth_all), bf16),
            pltpu.VMEM((n_tok, cols // 2), bf16),
            pltpu.VMEM((n_tok, cols // 2), f32),
            pltpu.VMEM((2 * n_s, n_tok, n_z * r), bf16),
            pltpu.VMEM((2 * team, n_z * r), bf16),
            pltpu.VMEM((n_z * r, 2 * team), bf16),
            pltpu.VMEM((PARTS, n_z * r, width), bf16),
            pltpu.VMEM((PARTS, team, width), bf16),
            pltpu.VMEM((PARTS, team, width), bf16),
            pltpu.VMEM((PARTS, team, width), bf16),
            pltpu.VMEM((PARTS, n_s, n_tok, width), bf16),
            pltpu.VMEM((team, width), f32),
            pltpu.VMEM((PARTS, n_tok, width), f32),
            pltpu.VMEM((PARTS, 2 * team, width), bf16),
            pltpu.VMEM((PARTS, r, width), f32),
            pltpu.VMEM((PARTS, n_z * r, width), bf16),
            pltpu.VMEM((PARTS, n_z, r, width), bf16),
            pltpu.VMEM((PARTS, n_g, r, width), bf16),
        ]
        + [dma((3,)), dma((PARTS, 2)), dma((PARTS, n_z)), dma((PARTS, n_z))]
        + [dma((2 * n_s,))] * 2
        + [dma((PARTS,))] * 2
        + [dma((PARTS, n_s))] * 6
        + [dma((PARTS, n_z))] * 2
        + [dma((PARTS, n_g))] * 2
        + [dma((PARTS, n_s, 2))] * 2,
        compiler_params=pltpu.CompilerParams(
            collective_id=0, has_side_effects=True, vmem_limit_bytes=60 * 1024 * 1024
        ),
        cost_estimate=pl.CostEstimate(
            flops=4 * n_tok * depth_all * cols,
            bytes_accessed=4 * depth * cols,
            transcendentals=n_tok * cols // 2,
        ),
    )(tokens, panel, cotangent)
    return hidden, grad.astype(jnp.float32)


def solution(mesh):
    placed = (P(("dp", "tensor"), None), P("tensor", None), P(("dp", "tensor"), None))
    return jax.shard_map(
        on_device,
        mesh=mesh,
        in_specs=placed,
        out_specs=(P(("dp", "tensor"), None), P("tensor", None)),
        check_vma=False,
    )
```
